128 devices in a mesh: batch: 16 (over x, y), proto: 8 (over z, core).
Axes of the slice: x: 4, y: 4, z: 4, core: 2. Of those that a mesh axis runs over, the one named last changes fastest.
Arguments:
- teacher_feats: bfloat16 [6144, 256], P('batch'), may hold values from -6 to 6
- student_feats: bfloat16 [6144, 256], P('batch'), may hold values from -6 to 6
- proto_weight: bfloat16 [256, 131072], P(None, 'proto'), may hold values from -1 to 1
Outputs:
- feat_grad: float32 [6144, 256], P('batch')
- proto_grad: float32 [256, 131072], P(None, ('proto', 'batch'))
The draws below stay inside these ranges and needn't reach their ends.
All inputs are finite; a program needn't handle non-finite values.
Results may differ from the reference program's by a relative error of at most 0.0005.
The reference program's roundings to bfloat16 on the way (of `protos`, `teach`, `stud` and `grad_s`) count: a program that leaves them out, or rounds other values in their place, can miss the bound.
Values may be sent and summed in bfloat16 or wider, within the bound.
No kernel may reach another device: no remote copies, remote signals or barrier semaphores. Data moves between devices by JAX's collectives and lax.ppermute only.
A program may use at most 192 MiB of HBM per device.

```python
import math
import jax
import jax.numpy as jnp
from jax import lax

D = 256
PROTOS = 131072
ITERS = 3
ROWS_DEV = 384
CROPS = 6144
N_PROTO = 8


def cluster_dirs(key):
    return jax.random.normal(jax.random.fold_in(key, 101), (16, D), jnp.float32)


def draw_teacher_feats(key, part):
    dirs = cluster_dirs(key)
    key = jax.random.fold_in(key, 3)
    keys = jax.random.split(key, 5)
    nblk = CROPS // ROWS_DEV
    block_dir = jax.random.normal(keys[0], (nblk, D), jnp.float32)
    base = jax.random.randint(keys[1], (nblk,), 0, 16)
    which = (jnp.repeat(base, ROWS_DEV) + jax.random.randint(keys[2], (CROPS,), 0, 8)) % 16
    noise = jax.random.normal(keys[3], (CROPS, D), jnp.float32)
    strength = jax.random.uniform(keys[4], (CROPS, 1), jnp.float32, 0.7, 1.5)
    block_amp = 1.2
    rows = noise + strength * dirs[which] + block_amp * jnp.repeat(block_dir, ROWS_DEV, axis=0)
    return jnp.clip(rows, -6.0, 6.0).astype(jnp.bfloat16)


def draw_proto_weight(key, part):
    dirs = cluster_dirs(key)
    key = jax.random.fold_in(key, 5)
    keys = jax.random.split(key, 4)
    which = jax.random.randint(keys[0], (PROTOS,), 0, 16)
    attached = jax.random.randint(keys[1], (PROTOS,), 0, 2).astype(jnp.float32)
    noise = jax.random.normal(keys[2], (D, PROTOS), jnp.float32)
    strength = attached * jax.random.uniform(keys[3], (PROTOS,), jnp.float32, 0.5, 1.0)
    cols = 0.25 * (noise + strength[None, :] * dirs[which].T)
    return jnp.clip(cols, -1.0, 1.0).astype(jnp.bfloat16)


def shard_levels(rng, extent, shards, least, high):
    def one(dim, blocks):
        steps = jax.random.uniform(jax.random.fold_in(jax.random.fold_in(rng, 6), dim), (blocks,), jnp.float32, least / len(shards), high / len(shards))
        return jnp.repeat(jnp.exp(steps), extent[dim] // blocks).reshape((-1,) + (1,) * (len(extent) - dim - 1))

    gain = one(*shards[0])
    for cut in shards[1:]:
        gain = gain * one(*cut)
    return gain


def normal_values(key, dims, scale, reach, cuts=(), held_as=jnp.bfloat16):
    drawn = jax.random.normal(key, dims, jnp.float32) * scale
    if len(cuts) > 0:
        drawn = shard_levels(key, dims, cuts, -0.22, 0.18) * drawn
    return jnp.clip(drawn, min=-reach, max=reach).astype(held_as)


def setup_inputs(seed: int = 0) -> dict:
    streams_of = jax.random.split(jax.random.key(seed), 4)
    teacher_feats = draw_teacher_feats(jax.random.fold_in(streams_of[3], 71), 0)
    student_feats = normal_values(streams_of[1], (CROPS, D), 1.0, 6.0, ((0, 16),))
    proto_weight = draw_proto_weight(jax.random.fold_in(streams_of[3], 71), 0)
    return {"teacher_feats": teacher_feats, "student_feats": student_feats, "proto_weight": proto_weight}


def unit_rows(feats):
    feats_f = feats.astype(jnp.float32)
    rnorm = lax.rsqrt(lax.optimization_barrier(jnp.mean(feats_f * feats_f, axis=1, keepdims=True)) + 1e-06) / math.sqrt(D)
    return (feats_f * rnorm, rnorm)

def reference(teacher_feats, student_feats, proto_weight):
    weight_f = proto_weight.astype(jnp.float32)
    protos = (weight_f * lax.rsqrt(lax.optimization_barrier(jnp.mean(weight_f * weight_f, axis=0, keepdims=True)) + 1e-06) / math.sqrt(D)).astype(jnp.bfloat16)
    teach_f, unused = unit_rows(teacher_feats)
    teach = teach_f.astype(jnp.bfloat16)
    stud_f, rnorm_s = unit_rows(student_feats)
    stud = stud_f.astype(jnp.bfloat16)
    nblock = N_PROTO
    width = PROTOS // nblock
    blocks = protos.reshape(D, nblock, width).transpose(1, 0, 2)

    def teacher_exp(block):
        return jnp.exp(jnp.dot(teach, block, preferred_element_type=jnp.float32) / 0.07)

    def student_exp(block):
        return jnp.exp(jnp.dot(stud, block, preferred_element_type=jnp.float32) / 0.1)
    rowsc = jnp.ones((CROPS,), jnp.float32)
    zden = jnp.zeros((CROPS,), jnp.float32)
    colsc = jnp.zeros((nblock, width), jnp.float32)
    for step in range(ITERS):

        def sweep(carry, block):
            rows_acc, den_acc = carry
            expo = teacher_exp(block)
            col_factor = 1.0 / lax.optimization_barrier(jnp.sum(expo * rowsc[:, None], axis=0))
            rows_acc = rows_acc + lax.optimization_barrier(jnp.sum(expo * col_factor[None, :], axis=1))
            if step == 0:
                den_acc = den_acc + lax.optimization_barrier(jnp.sum(student_exp(block), axis=1))
            return ((rows_acc, den_acc), col_factor)
        (row_total, den_new), colsc = lax.scan(sweep, (jnp.zeros((CROPS,), jnp.float32), zden), blocks)
        if step == 0:
            zden = den_new
        rowsc = 1.0 / row_total

    def final(dz_acc, pair):
        block, col_factor = pair
        target = teacher_exp(block) * rowsc[:, None] * col_factor[None, :]
        prob = student_exp(block) / zden[:, None]
        grad_s = (PROTOS * (prob - target) / 0.1).astype(jnp.bfloat16)
        dz_acc = dz_acc + lax.dot_general(grad_s, block, (((1,), (1,)), ((), ())), preferred_element_type=jnp.float32)
        grad_w = lax.dot_general(stud, grad_s, (((0,), (0,)), ((), ())), preferred_element_type=jnp.float32)
        return (dz_acc, grad_w)
    dz, grads = lax.scan(final, jnp.zeros((CROPS, D), jnp.float32), (blocks, colsc))
    feat_grad = (dz - stud_f * lax.optimization_barrier(jnp.sum(stud_f * dz, axis=1, keepdims=True))) * rnorm_s
    proto_grad = grads.transpose(1, 0, 2).reshape(D, PROTOS)
    return (feat_grad, proto_grad)
```

```python
import math

import jax
import jax.numpy as jnp
from jax import lax
from jax.experimental import pallas as pl
from jax.experimental.pallas import tpu as pltpu
from jax.sharding import Mesh, PartitionSpec as P

D = 256
PROTOS = 131072
ITERS = 3
ROWS = 384
COLS = 16384
OWN = 1024
GROUPS = COLS // 128
NB = 16
NP = 8
KT = math.log2(math.e) / 0.07
KS = math.log2(math.e) / 0.1
GSCALE = PROTOS / 0.1

f32 = jnp.float32
bf16 = jnp.bfloat16
XY = ("x", "y")
ZC = ("z", "c")
MIB = 2**20


def whole():
    return pl.BlockSpec(memory_space=pltpu.VMEM)


def params(mib):
    return pltpu.CompilerParams(vmem_limit_bytes=mib * MIB)


def row_norm(feats):
    return lax.rsqrt(jnp.mean(feats * feats, axis=1, keepdims=True) + 1e-06) / math.sqrt(D)


def lanes_to_rows(vec, width):
    return jnp.transpose(jnp.broadcast_to(vec, (width, vec.shape[1])))


def rows_to_lanes(acc):
    return jnp.sum(jnp.transpose(acc), axis=0, keepdims=True)


def norm_kernel(t_ref, s_ref, t_out, s_out):
    for src, dst in ((t_ref, t_out), (s_ref, s_out)):
        feats = src[...].astype(f32)
        dst[...] = (feats * row_norm(feats)).astype(bf16)


def first_kernel(w_ref, t_ref, s_ref, p_ref, e_ref, col_ref, z_ref, zacc):
    step = pl.program_id(0)

    @pl.when(step == 0)
    def _():
        zacc[...] = jnp.zeros_like(zacc)

    w = w_ref[...].astype(f32)
    inv = lax.rsqrt(jnp.mean(w * w, axis=0, keepdims=True) + 1e-06) / math.sqrt(D)
    p_ref[...] = (w * inv).astype(bf16)
    sums = []
    zsum = zacc[...]
    for n in range(4):
        p = p_ref[:, n * 256 : (n + 1) * 256]
        e = jnp.exp2(jnp.dot(t_ref[...], p, preferred_element_type=f32) * KT)
        e_ref[:, pl.ds(pl.multiple_of(step * 1024 + n * 256, 256), 256)] = e
        for h in range(2):
            sums.append(jnp.sum(e[:, h * 128 : (h + 1) * 128], axis=0, keepdims=True))
        s = jnp.exp2(jnp.dot(s_ref[...], p, preferred_element_type=f32) * KS)
        zsum = zsum + s[:, :128] + s[:, 128:]
    zacc[...] = zsum
    part = jnp.concatenate(sums, axis=0)
    col_ref[:, pl.ds(pl.multiple_of(step * 8, 8), 8), :] = jnp.broadcast_to(part, (NB, 8, 128))

    @pl.when(step == pl.num_programs(0) - 1)
    def _():
        z_ref[...] = rows_to_lanes(zacc[...])


def row_pass(colp_ref, e_ref, c_ref):
    c_ref[...] = 1.0 / jnp.sum(colp_ref[...], axis=0)
    halves = []
    for half in range(2):
        rows = slice(half * 192, (half + 1) * 192)

        def body(q, acc):
            c8 = c_ref[pl.ds(pl.multiple_of(q * 8, 8), 8), :]
            for u in range(8):
                e = e_ref[rows, pl.ds(pl.multiple_of(q * 1024 + u * 128, 128), 128)]
                acc = acc + e * c8[u : u + 1, :]
            return acc

        halves.append(lax.fori_loop(0, GROUPS // 8, body, jnp.zeros((192, 128), f32)))
    return rows_to_lanes(jnp.concatenate(halves, axis=0))


def row_z_kernel(colp_ref, z_ref, e_ref, c_ref, row_ref):
    row = row_pass(colp_ref, e_ref, c_ref)
    both = jnp.concatenate([row, z_ref[...]], axis=0)
    row_ref[...] = jnp.broadcast_to(both, (NP, 2, ROWS))


def row_kernel(colp_ref, e_ref, c_ref, row_ref):
    row = row_pass(colp_ref, e_ref, c_ref)
    row_ref[...] = jnp.broadcast_to(row, (NP, 1, ROWS))


def col_kernel(rowp_ref, e_ref, col_ref, rb):
    rb[...] = lanes_to_rows(1.0 / jnp.sum(rowp_ref[:, 0, :], axis=0, keepdims=True), 128)

    @pl.loop(0, GROUPS // 8)
    def _(q):
        accs = [jnp.zeros((8, 128), f32) for _ in range(8)]
        for i in range(ROWS // 8):
            r = rb[i * 8 : (i + 1) * 8, :]
            e = e_ref[i * 8 : (i + 1) * 8, pl.ds(pl.multiple_of(q * 1024, 1024), 1024)]
            for u in range(8):
                accs[u] = accs[u] + e[:, u * 128 : (u + 1) * 128] * r
        part = jnp.concatenate([jnp.sum(a, axis=0, keepdims=True) for a in accs], axis=0)
        col_ref[:, pl.ds(pl.multiple_of(q * 8, 8), 8), :] = jnp.broadcast_to(part, (NB, 8, 128))


def dz_kernel(rz_ref, c_ref, s_ref, e_ref, p_ref, dz_ref, rb, zb):
    step = pl.program_id(0)

    @pl.when(step == 0)
    def _():
        rb[...] = lanes_to_rows(rz_ref[0:1, :], 128)
        zb[...] = lanes_to_rows(rz_ref[1:2, :], 128)
        dz_ref[...] = jnp.zeros_like(dz_ref)

    c8 = c_ref[pl.ds(pl.multiple_of(step * 8, 8), 8), :]
    r = rb[...]
    z = zb[...]
    acc = dz_ref[...]
    for n in range(4):
        p = p_ref[:, n * 256 : (n + 1) * 256]
        s = jnp.exp2(jnp.dot(s_ref[...], p, preferred_element_type=f32) * KS)
        e = e_ref[:, pl.ds(pl.multiple_of(step * 1024 + n * 256, 256), 256)]
        parts = []
        for h in range(2):
            lane = slice(h * 128, (h + 1) * 128)
            u = n * 2 + h
            parts.append((s[:, lane] * z - e[:, lane] * r * c8[u : u + 1, :]).astype(bf16))
        g = jnp.concatenate(parts, axis=1)
        acc = acc + lax.dot_general(g, p, (((1,), (1,)), ((), ())), preferred_element_type=f32)
    dz_ref[...] = acc


def pg_kernel(rz_ref, c_ref, p_ref, t_ref, s_ref, out_ref, pt, cb, acc):
    step = pl.program_id(0)

    @pl.when(step == 0)
    def _():
        pt[...] = jnp.transpose(p_ref[...].astype(f32)).astype(bf16)
        for q in range(8):
            cb[q * 128 : (q + 1) * 128, :] = lanes_to_rows(c_ref[q : q + 1, :], 128)
        acc[...] = jnp.zeros_like(acc)

    t = t_ref[...]
    s = s_ref[...]
    r = jnp.concatenate([rz_ref[0, 0:1, :], rz_ref[1, 0:1, :]], axis=1)
    z = jnp.concatenate([rz_ref[0, 1:2, :], rz_ref[1, 1:2, :]], axis=1)
    nt = (((1,), (1,)), ((), ()))
    for m in range(4):
        rows = slice(m * 256, (m + 1) * 256)
        pm = pt[rows, :]
        c = cb[rows, :]
        et = jnp.exp2(lax.dot_general(pm, t, nt, preferred_element_type=f32) * KT)
        es = jnp.exp2(lax.dot_general(pm, s, nt, preferred_element_type=f32) * KS)
        parts = []
        for k in range(6):
            lane = slice(k * 128, (k + 1) * 128)
            parts.append((es[:, lane] * z[:, lane] - et[:, lane] * r[:, lane] * c).astype(bf16))
        g = jnp.concatenate(parts, axis=1)
        acc[rows, :] += jnp.dot(g, s, preferred_element_type=f32)

    @pl.when(step == pl.num_programs(0) - 1)
    def _():
        out_ref[...] = jnp.transpose(acc[...])


def in_vmem(x):
    return pltpu.with_memory_space_constraint(x, pltpu.VMEM)


def exchange(x, axes):
    return lax.all_to_all(x, axes, 0, 0, tiled=True)


def sum_over_z(x):
    parts = [x]
    for d in (1, 2, 3):
        parts.append(lax.ppermute(x, "z", [(i, (i + d) % 4) for i in range(4)]))
    return parts


def shards(teacher_feats, student_feats, proto_weight):
    core = lax.axis_index("c")
    block = lax.axis_index("x") * 4 + lax.axis_index("y")
    sds = jax.ShapeDtypeStruct

    teach, stud = pl.pallas_call(
        norm_kernel,
        out_shape=(sds((ROWS, D), bf16), sds((ROWS, D), bf16)),
        in_specs=[whole()] * 2,
        out_specs=(whole(), whole()),
        compiler_params=params(8),
        name="norm",
    )(teacher_feats, student_feats)
    teach_all = lax.all_gather(teach, XY, axis=0, tiled=True)
    stud_all = lax.all_gather(stud, XY, axis=0, tiled=True)

    protos, expo, colp, zpart = pl.pallas_call(
        first_kernel,
        grid=(COLS // 1024,),
        out_shape=(
            sds((D, COLS), bf16),
            pltpu.VMEM((ROWS, COLS), f32),
            sds((NB, GROUPS, 128), f32),
            sds((1, ROWS), f32),
        ),
        in_specs=[pl.BlockSpec((D, 1024), lambda i: (0, i)), whole(), whole()],
        out_specs=(pl.BlockSpec((D, 1024), lambda i: (0, i)), whole(), whole(), whole()),
        scratch_shapes=[pltpu.VMEM((ROWS, 128), f32)],
        compiler_params=params(16),
        name="first",
    )(proto_weight, teach, stud)

    row_out = (sds((GROUPS, 128), f32), sds((NP, 1, ROWS), f32))
    row_out_z = (sds((GROUPS, 128), f32), sds((NP, 2, ROWS), f32))
    for step in range(ITERS):
        colp = exchange(colp, XY)
        if step == 0:
            colsc, rowp = pl.pallas_call(
                row_z_kernel,
                out_shape=row_out_z,
                in_specs=[whole()] * 3,
                out_specs=(whole(), whole()),
                compiler_params=params(8),
                name="row_z",
            )(colp, zpart, in_vmem(expo))
        else:
            colsc, rowp = pl.pallas_call(
                row_kernel,
                out_shape=row_out,
                in_specs=[whole()] * 2,
                out_specs=(whole(), whole()),
                compiler_params=params(8),
                name="row",
            )(colp, in_vmem(expo))
        rowp = exchange(rowp, ZC)
        if step == 0:
            zinv = GSCALE / jnp.sum(rowp[:, 1, :], axis=0, keepdims=True)
        if step < ITERS - 1:
            colp = pl.pallas_call(
                col_kernel,
                out_shape=sds((NB, GROUPS, 128), f32),
                in_specs=[whole()] * 2,
                out_specs=whole(),
                scratch_shapes=[pltpu.VMEM((ROWS, 128), f32)],
                compiler_params=params(8),
                name="col",
            )(rowp, in_vmem(expo))

    rowsc = GSCALE / jnp.sum(rowp[:, 0, :], axis=0, keepdims=True)
    rz = jnp.concatenate([rowsc, zinv], axis=0)
    rz_all = exchange(jnp.broadcast_to(rz[None], (NB, 2, ROWS)), XY)

    dz_part = pl.pallas_call(
        dz_kernel,
        grid=(COLS // 1024,),
        out_shape=sds((ROWS, D), f32),
        in_specs=[whole()] * 4 + [pl.BlockSpec((D, 1024), lambda i: (0, i))],
        out_specs=whole(),
        scratch_shapes=[pltpu.VMEM((ROWS, 128), f32)] * 2,
        compiler_params=params(12),
        name="dz",
    )(rz, colsc, stud, in_vmem(expo), protos)

    half = ROWS // 2
    mine = lax.dynamic_slice(dz_part, (core * half, 0), (half, D))
    other = lax.dynamic_slice(dz_part, ((1 - core) * half, 0), (half, D))
    got = lax.ppermute(other, "c", [(0, 1), (1, 0)])
    parts = sum_over_z(mine + got)

    proto_grad = pl.pallas_call(
        pg_kernel,
        grid=(8,),
        out_shape=sds((D, OWN), f32),
        in_specs=[
            pl.BlockSpec((2, 2, ROWS), lambda i: (i, 0, 0)),
            whole(),
            whole(),
            pl.BlockSpec((2 * ROWS, D), lambda i: (i, 0)),
            pl.BlockSpec((2 * ROWS, D), lambda i: (i, 0)),
        ],
        out_specs=whole(),
        scratch_shapes=[
            pltpu.VMEM((OWN, D), bf16),
            pltpu.VMEM((OWN, 128), f32),
            pltpu.VMEM((OWN, D), f32),
        ],
        compiler_params=params(24),
        cost_estimate=pl.CostEstimate(flops=9700000000, bytes_accessed=8000000, transcendentals=12600000),
        name="pg",
    )(
        rz_all,
        lax.dynamic_slice(colsc, (block * 8, 0), (8, 128)),
        lax.dynamic_slice(protos, (0, block * OWN), (D, OWN)),
        teach_all,
        stud_all,
    )

    dz = (parts[0] + parts[2]) + (parts[1] + parts[3])
    feats = lax.dynamic_slice(student_feats, (core * half, 0), (half, D)).astype(f32)
    rnorm = row_norm(feats)
    stud_f = feats * rnorm
    grad = (dz - stud_f * jnp.sum(stud_f * dz, axis=1, keepdims=True)) * rnorm
    sibling = lax.ppermute(grad, "c", [(0, 1), (1, 0)])
    feat_grad = jnp.where(
        core == 0,
        jnp.concatenate([grad, sibling], axis=0),
        jnp.concatenate([sibling, grad], axis=0),
    )
    return (feat_grad, proto_grad)


def solution(mesh):
    grid = Mesh(mesh.devices.reshape(4, 4, 4, 2), ("x", "y", "z", "c"))
    in_specs = (P(XY, None), P(XY, None), P(None, ZC))
    out_specs = (P(XY, None), P(None, ZC + XY))
    return jax.shard_map(shards, mesh=grid, in_specs=in_specs, out_specs=out_specs, check_vma=False)
```

```python
import math

import jax
import jax.numpy as jnp
from jax import lax
from jax.experimental import pallas as pl
from jax.experimental.pallas import tpu as pltpu
from jax.sharding import Mesh, PartitionSpec as P

D = 256
PROTOS = 131072
ITERS = 3
ROWS = 384
COLS = 16384
OWN = 1024
SHARE = 48
BLOCK = 4096
PG_ROWS = 1536
GROUPS = COLS // 128
NB = 16
NP = 8
ND = 128
KT = math.log2(math.e) / 0.07
KS = math.log2(math.e) / 0.1
GSCALE = PROTOS / 0.1

f32 = jnp.float32
bf16 = jnp.bfloat16
XY = ("x", "y")
ZC = ("z", "c")
ALL = XY + ZC
MIB = 2**20


def whole():
    return pl.BlockSpec(memory_space=pltpu.VMEM)


def params(mib):
    return pltpu.CompilerParams(vmem_limit_bytes=mib * MIB)


def row_norm(feats):
    return lax.rsqrt(jnp.mean(feats * feats, axis=1, keepdims=True) + 1e-06) / math.sqrt(D)


def lanes_to_rows(vec, width):
    return jnp.transpose(jnp.broadcast_to(vec, (width, vec.shape[1])))


def rows_to_lanes(acc):
    return jnp.sum(jnp.transpose(acc), axis=0, keepdims=True)


def norm_kernel(t_ref, s_ref, out_ref, share_ref):
    for src, rows in ((t_ref, slice(0, ROWS)), (s_ref, slice(ROWS, 2 * ROWS))):
        feats = src[...].astype(f32)
        out_ref[rows, :] = (feats * row_norm(feats)).astype(bf16)
    start = (lax.axis_index("z") * 2 + lax.axis_index("c")) * SHARE
    for k in range(2):
        rows = pl.ds(pl.multiple_of(k * ROWS + start, SHARE), SHARE)
        share_ref[:, k * D : (k + 1) * D] = out_ref[rows, :]


def first_kernel(w_ref, f_ref, p_ref, e_ref, col_ref, z_ref, zacc):
    step = pl.program_id(0)

    @pl.when(step == 0)
    def _():
        zacc[...] = jnp.zeros_like(zacc)

    sums = []
    zsum = zacc[...]
    for n in range(BLOCK // 256):
        lanes = slice(n * 256, (n + 1) * 256)
        w = w_ref[:, lanes].astype(f32)
        inv = lax.rsqrt(jnp.mean(w * w, axis=0, keepdims=True) + 1e-06) / math.sqrt(D)
        p = (w * inv).astype(bf16)
        p_ref[:, lanes] = p
        x = jnp.dot(f_ref[...], p, preferred_element_type=f32)
        e = jnp.exp2(x[:ROWS] * KT)
        e_ref[:, pl.ds(pl.multiple_of(step * BLOCK + n * 256, 256), 256)] = e
        for h in range(2):
            sums.append(jnp.sum(e[:, h * 128 : (h + 1) * 128], axis=0, keepdims=True))
        s = jnp.exp2(x[ROWS:] * KS)
        zsum = zsum + s[:, :128] + s[:, 128:]
    zacc[...] = zsum
    part = jnp.concatenate(sums, axis=0)
    tall = BLOCK // 128
    col_ref[:, pl.ds(pl.multiple_of(step * tall, tall), tall), :] = jnp.broadcast_to(
        part, (NB, tall, 128)
    )

    @pl.when(step == pl.num_programs(0) - 1)
    def _():
        z_ref[...] = rows_to_lanes(zacc[...])


def row_pass(colp_ref, e_ref, c_ref, acc_ref):
    c_ref[...] = 1.0 / jnp.sum(colp_ref[...], axis=0)
    tiles = 12

    @pl.loop(0, ROWS // (8 * tiles))
    def _(k):
        base = pl.multiple_of(k * 8 * tiles, 8 * tiles)

        def body(q, accs):
            c8 = c_ref[pl.ds(pl.multiple_of(q * 8, 8), 8), :]
            cs = [jnp.broadcast_to(c8[u : u + 1, :], (8, 128)) for u in range(8)]
            out = []
            for i in range(tiles):
                e = e_ref[
                    pl.ds(pl.multiple_of(base + i * 8, 8), 8),
                    pl.ds(pl.multiple_of(q * 1024, 1024), 1024),
                ]
                p = [e[:, u * 128 : (u + 1) * 128] * cs[u] for u in range(8)]
                while len(p) > 1:
                    p = [p[m] + p[m + 1] for m in range(0, len(p), 2)]
                out.append(accs[i] + p[0])
            return tuple(out)

        zero = jnp.zeros((8, 128), f32)
        accs = lax.fori_loop(0, GROUPS // 8, body, (zero,) * tiles)
        for i in range(tiles):
            acc_ref[pl.ds(pl.multiple_of(base + i * 8, 8), 8), :] = accs[i]

    return rows_to_lanes(acc_ref[...])


def last_row_kernel(colp_ref, z_ref, e_ref, c_ref, row_ref, kept_ref, acc):
    row = row_pass(colp_ref, e_ref, c_ref, acc)
    both = jnp.concatenate([row, z_ref[...]], axis=0)
    row_ref[...] = jnp.broadcast_to(both, (ND, 2, ROWS))


def row_kernel(colp_ref, e_ref, c_ref, row_ref, kept_ref, acc):
    row = row_pass(colp_ref, e_ref, c_ref, acc)
    row_ref[...] = jnp.broadcast_to(row, (NP, 1, ROWS))


def col_kernel(rowp_ref, e_ref, col_ref, kept_ref, rb):
    rb[...] = lanes_to_rows(1.0 / jnp.sum(rowp_ref[:, 0, :], axis=0, keepdims=True), 128)

    @pl.loop(0, GROUPS // 8)
    def _(q):
        accs = [jnp.zeros((8, 128), f32) for _ in range(8)]
        for i in range(ROWS // 8):
            r = rb[i * 8 : (i + 1) * 8, :]
            e = e_ref[i * 8 : (i + 1) * 8, pl.ds(pl.multiple_of(q * 1024, 1024), 1024)]
            for u in range(8):
                accs[u] = accs[u] + e[:, u * 128 : (u + 1) * 128] * r
        part = jnp.concatenate([jnp.sum(a, axis=0, keepdims=True) for a in accs], axis=0)
        col_ref[:, pl.ds(pl.multiple_of(q * 8, 8), 8), :] = jnp.broadcast_to(part, (NB, 8, 128))


def dz_kernel(rzp_ref, c_ref, f_ref, e_ref, p_ref, mine_ref, other_ref, rz_ref, rb, zb, dz_ref):
    step = pl.program_id(0)

    @pl.when(step == 0)
    def _():
        block = lax.axis_index("x") * 4 + lax.axis_index("y")
        for b in range(NB):
            rz_ref[b] = GSCALE / jnp.sum(rzp_ref[b * NP : (b + 1) * NP], axis=0)
        rz = rz_ref[block]
        rb[...] = lanes_to_rows(rz[0:1, :], 128)
        zb[...] = lanes_to_rows(rz[1:2, :], 128)
        dz_ref[...] = jnp.zeros_like(dz_ref)

    tall = BLOCK // 128
    cs = c_ref[pl.ds(pl.multiple_of(step * tall, tall), tall), :]
    r = rb[...]
    z = zb[...]
    acc = dz_ref[...]
    for n in range(BLOCK // 256):
        p = p_ref[:, n * 256 : (n + 1) * 256]
        s = jnp.exp2(jnp.dot(f_ref[ROWS:, :], p, preferred_element_type=f32) * KS)
        e = e_ref[:, pl.ds(pl.multiple_of(step * BLOCK + n * 256, 256), 256)]
        parts = []
        for h in range(2):
            lane = slice(h * 128, (h + 1) * 128)
            u = n * 2 + h
            parts.append((s[:, lane] * z - e[:, lane] * r * cs[u : u + 1, :]).astype(bf16))
        g = jnp.concatenate(parts, axis=1)
        acc = acc + lax.dot_general(g, p, (((1,), (1,)), ((), ())), preferred_element_type=f32)
    dz_ref[...] = acc

    @pl.when(step == pl.num_programs(0) - 1)
    def _():
        half = ROWS // 2
        core = lax.axis_index("c")
        mine_ref[...] = dz_ref[pl.ds(pl.multiple_of(core * half, half), half), :]
        other_ref[...] = dz_ref[pl.ds(pl.multiple_of((1 - core) * half, half), half), :]


def pg_kernel(block_ref, rz_ref, c_ref, p_ref, f_ref, out_ref, pt, cb, acc, g):
    step = pl.program_id(0)

    @pl.when(step == 0)
    def _():
        pt[...] = jnp.transpose(p_ref[...].astype(f32)).astype(bf16)
        for q in range(8):
            cb[q * 128 : (q + 1) * 128, :] = lanes_to_rows(c_ref[q : q + 1, :], 128)
        acc[...] = jnp.zeros_like(acc)

    t = f_ref[:, :D]
    s = f_ref[:, D:]
    blocks = range(PG_ROWS // ROWS)
    r = jnp.concatenate([rz_ref[b, 0:1, :] for b in blocks], axis=1)
    z = jnp.concatenate([rz_ref[b, 1:2, :] for b in blocks], axis=1)
    nt = (((1,), (1,)), ((), ()))
    for n in range(PG_ROWS // 256):
        rows = slice(n * 256, (n + 1) * 256)
        et = jnp.exp2(lax.dot_general(pt[...], t[rows], nt, preferred_element_type=f32) * KT)
        es = jnp.exp2(lax.dot_general(pt[...], s[rows], nt, preferred_element_type=f32) * KS)
        for h in range(2):
            lane = slice(h * 128, (h + 1) * 128)
            to = slice(n * 256 + h * 128, n * 256 + (h + 1) * 128)
            g[:, to] = (es[:, lane] * z[:, to] - et[:, lane] * r[:, to] * cb[...]).astype(bf16)
    acc[...] += jnp.dot(g[...], s, preferred_element_type=f32)

    @pl.when(step == pl.num_programs(0) - 1)
    def _():
        out_ref[...] = jnp.transpose(acc[...])


def in_vmem(x):
    return pltpu.with_memory_space_constraint(x, pltpu.VMEM)


def in_hbm(x):
    return pltpu.with_memory_space_constraint(x, pltpu.HBM)


def exchange(x, axes):
    return lax.all_to_all(x, axes, 0, 0, tiled=True)


def sum_over_z(x):
    parts = [x]
    for d in (1, 2, 3):
        parts.append(lax.ppermute(x, "z", [(i, (i + d) % 4) for i in range(4)]))
    return parts


def shards(teacher_feats, student_feats, proto_weight):
    core = lax.axis_index("c")
    block = lax.axis_index("x") * 4 + lax.axis_index("y")
    sds = jax.ShapeDtypeStruct
    vmem = pltpu.VMEM
    kept = vmem((ROWS, COLS), f32)

    feats, share = pl.pallas_call(
        norm_kernel,
        grid=(1,),
        out_shape=(vmem((2 * ROWS, D), bf16), sds((SHARE, 2 * D), bf16)),
        in_specs=[pl.BlockSpec((ROWS, D), lambda i: (0, 0))] * 2,
        out_specs=(whole(), whole()),
        compiler_params=params(14),
        name="norm",
    )(in_hbm(teacher_feats), in_hbm(student_feats))
    feats_all = lax.all_gather(share, ALL, axis=0, tiled=True)

    protos, expo, colp, zpart = pl.pallas_call(
        first_kernel,
        grid=(COLS // BLOCK,),
        out_shape=(
            pltpu.HBM((D, COLS), bf16),
            kept,
            vmem((NB, GROUPS, 128), f32),
            vmem((1, ROWS), f32),
        ),
        in_specs=[pl.BlockSpec((D, BLOCK), lambda i: (0, i)), whole()],
        out_specs=(pl.BlockSpec((D, BLOCK), lambda i: (0, i)), whole(), whole(), whole()),
        scratch_shapes=[vmem((ROWS, 128), f32)],
        compiler_params=params(14),
        name="first",
    )(in_hbm(proto_weight), in_vmem(feats))

    for step in range(ITERS):
        colp = in_vmem(exchange(colp, XY))
        if step == ITERS - 1:
            break
        unused, rowp, expo = pl.pallas_call(
            row_kernel,
            out_shape=(vmem((GROUPS, 128), f32), vmem((NP, 1, ROWS), f32), kept),
            in_specs=[whole()] * 2,
            out_specs=(whole(),) * 3,
            input_output_aliases={1: 2},
            scratch_shapes=[vmem((ROWS, 128), f32)],
            compiler_params=params(14),
            name="row",
        )(colp, in_vmem(expo))
        rowp = in_vmem(exchange(rowp, ZC))
        colp, expo = pl.pallas_call(
            col_kernel,
            out_shape=(vmem((NB, GROUPS, 128), f32), kept),
            in_specs=[whole()] * 2,
            out_specs=(whole(), whole()),
            input_output_aliases={1: 1},
            scratch_shapes=[vmem((ROWS, 128), f32)],
            compiler_params=params(14),
            name="col",
        )(rowp, in_vmem(expo))

    colsc, rzp, expo = pl.pallas_call(
        last_row_kernel,
        out_shape=(vmem((GROUPS, 128), f32), vmem((ND, 2, ROWS), f32), kept),
        in_specs=[whole()] * 3,
        out_specs=(whole(),) * 3,
        input_output_aliases={2: 2},
        scratch_shapes=[vmem((ROWS, 128), f32)],
        compiler_params=params(14),
        name="row_last",
    )(colp, in_vmem(zpart), in_vmem(expo))
    rzp = in_vmem(exchange(rzp, ALL))

    half = ROWS // 2
    mine, other, rz_all = pl.pallas_call(
        dz_kernel,
        grid=(COLS // BLOCK,),
        out_shape=(vmem((half, D), f32), vmem((half, D), f32), sds((NB, 2, ROWS), f32)),
        in_specs=[whole()] * 4 + [pl.BlockSpec((D, BLOCK), lambda i: (0, i))],
        out_specs=(whole(), whole(), whole()),
        scratch_shapes=[vmem((ROWS, 128), f32)] * 2 + [vmem((ROWS, D), f32)],
        compiler_params=params(14),
        name="dz",
    )(rzp, in_vmem(colsc), in_vmem(feats), in_vmem(expo), in_hbm(protos))

    got = lax.ppermute(other, "c", [(0, 1), (1, 0)])
    parts = sum_over_z(mine + got)

    proto_grad = pl.pallas_call(
        pg_kernel,
        grid_spec=pltpu.PrefetchScalarGridSpec(
            num_scalar_prefetch=1,
            grid=(NB * ROWS // PG_ROWS,),
            in_specs=[
                pl.BlockSpec((PG_ROWS // ROWS, 2, ROWS), lambda i, b: (i, 0, 0)),
                pl.BlockSpec((8, 128), lambda i, b: (b[0], 0)),
                pl.BlockSpec((D, OWN), lambda i, b: (0, b[0])),
                pl.BlockSpec((PG_ROWS, 2 * D), lambda i, b: (i, 0)),
            ],
            out_specs=pl.BlockSpec((D, OWN), lambda i, b: (0, 0)),
            scratch_shapes=[
                vmem((OWN, D), bf16),
                vmem((OWN, 128), f32),
                vmem((OWN, D), f32),
                vmem((OWN, PG_ROWS), bf16),
            ],
        ),
        out_shape=sds((D, OWN), f32),
        compiler_params=params(14),
        cost_estimate=pl.CostEstimate(flops=9700000000, bytes_accessed=8000000, transcendentals=12600000),
        name="pg",
    )(block.reshape(1), rz_all, colsc, in_hbm(protos), in_hbm(feats_all))

    parts, proto_grad, student_feats = lax.optimization_barrier(
        (parts, proto_grad, student_feats)
    )
    dz = (parts[0] + parts[2]) + (parts[1] + parts[3])
    feats = lax.dynamic_slice(student_feats, (core * half, 0), (half, D)).astype(f32)
    rnorm = row_norm(feats)
    stud_f = feats * rnorm
    grad = (dz - stud_f * jnp.sum(stud_f * dz, axis=1, keepdims=True)) * rnorm
    sibling = lax.ppermute(grad, "c", [(0, 1), (1, 0)])
    feat_grad = jnp.where(
        core == 0,
        jnp.concatenate([grad, sibling], axis=0),
        jnp.concatenate([sibling, grad], axis=0),
    )
    return (feat_grad, proto_grad)


def solution(mesh):
    grid = Mesh(mesh.devices.reshape(4, 4, 4, 2), ("x", "y", "z", "c"))
    in_specs = (P(XY, None), P(XY, None), P(None, ZC))
    out_specs = (P(XY, None), P(None, ZC + XY))
    return jax.shard_map(shards, mesh=grid, in_specs=in_specs, out_specs=out_specs, check_vma=False)
```

```python
import math

import jax
import jax.numpy as jnp
from jax import lax
from jax.experimental import pallas as pl
from jax.experimental.pallas import tpu as pltpu
from jax.sharding import Mesh, PartitionSpec as P

D = 256
PROTOS = 131072
ITERS = 3
ROWS = 384
COLS = 16384
OWN = 1024
SHARE = 48
BLOCK = 4096
PG_ROWS = 1536
GROUPS = COLS // 128
NB = 16
KT = math.log2(math.e) / 0.07
KS = math.log2(math.e) / 0.1
GSCALE = PROTOS / 0.1

f32 = jnp.float32
bf16 = jnp.bfloat16
XY = ("x", "y")
ZC = ("z", "c")
ALL = XY + ZC
MIB = 2**20


def whole():
    return pl.BlockSpec(memory_space=pltpu.VMEM)


def params(mib):
    return pltpu.CompilerParams(vmem_limit_bytes=mib * MIB)


def row_norm(feats):
    return lax.rsqrt(jnp.mean(feats * feats, axis=1, keepdims=True) + 1e-06) / math.sqrt(D)


def lanes_to_rows(vec, width):
    return jnp.transpose(jnp.broadcast_to(vec, (width, vec.shape[1])))


def rows_to_lanes(acc):
    return jnp.sum(jnp.transpose(acc), axis=0, keepdims=True)


def norm_kernel(t_ref, s_ref, out_ref, share_ref):
    for src, rows in ((t_ref, slice(0, ROWS)), (s_ref, slice(ROWS, 2 * ROWS))):
        feats = src[...].astype(f32)
        out_ref[rows, :] = (feats * row_norm(feats)).astype(bf16)
    start = (lax.axis_index("z") * 2 + lax.axis_index("c")) * SHARE
    for k in range(2):
        rows = pl.ds(pl.multiple_of(k * ROWS + start, SHARE), SHARE)
        share_ref[:, k * D : (k + 1) * D] = out_ref[rows, :]


def first_kernel(w_ref, f_ref, p_ref, e_ref, col_ref):
    step = pl.program_id(0)
    sums = []
    for n in range(BLOCK // 256):
        lanes = slice(n * 256, (n + 1) * 256)
        w = w_ref[:, lanes].astype(f32)
        inv = lax.rsqrt(jnp.mean(w * w, axis=0, keepdims=True) + 1e-06) / math.sqrt(D)
        p = (w * inv).astype(bf16)
        p_ref[:, lanes] = p
        e = jnp.exp2(jnp.dot(f_ref[:ROWS, :], p, preferred_element_type=f32) * KT)
        e_ref[:, pl.ds(pl.multiple_of(step * BLOCK + n * 256, 256), 256)] = e
        for h in range(2):
            sums.append(jnp.sum(e[:, h * 128 : (h + 1) * 128], axis=0, keepdims=True))
    tall = BLOCK // 128
    col_ref[pl.ds(pl.multiple_of(step * tall, tall), tall), :] = jnp.concatenate(sums, axis=0)


def z_kernel(after_ref, f_ref, p_ref, z_ref, zacc):
    step = pl.program_id(0)

    @pl.when(step == 0)
    def _():
        zacc[...] = jnp.zeros_like(zacc)

    zsum = zacc[...]
    for n in range(BLOCK // 256):
        p = p_ref[:, n * 256 : (n + 1) * 256]
        s = jnp.exp2(jnp.dot(f_ref[ROWS:, :], p, preferred_element_type=f32) * KS)
        zsum = zsum + s[:, :128] + s[:, 128:]
    zacc[...] = zsum

    @pl.when(step == pl.num_programs(0) - 1)
    def _():
        z_ref[...] = rows_to_lanes(zacc[...])


def sum_kernel(a_ref, b_ref, c_ref, d_ref, out_ref):
    out_ref[...] = (a_ref[...] + b_ref[...]) + (c_ref[...] + d_ref[...])


def pair_kernel(a_ref, b_ref, out_ref):
    out_ref[...] = a_ref[...] + b_ref[...]


def rz_kernel(a_ref, b_ref, c_ref, d_ref, out_ref):
    out_ref[...] = GSCALE / ((a_ref[...] + b_ref[...]) + (c_ref[...] + d_ref[...]))


def stack_kernel(a_ref, b_ref, c_ref, d_ref, other_ref, out_ref, kept_ref):
    for d, ref in enumerate((a_ref, b_ref, c_ref, d_ref)):
        out_ref[d] = ref[...]


def sum_z_kernel(a_ref, b_ref, c_ref, d_ref, z_ref, out_ref, z_out):
    out_ref[...] = (a_ref[...] + b_ref[...]) + (c_ref[...] + d_ref[...])
    z_out[...] = z_ref[...]


def row_pass(cols, e_ref, c_ref, acc_ref):
    c_ref[...] = 1.0 / ((cols[0][...] + cols[1][...]) + (cols[2][...] + cols[3][...]))
    tiles = 12

    @pl.loop(0, ROWS // (8 * tiles))
    def _(k):
        base = pl.multiple_of(k * 8 * tiles, 8 * tiles)

        def body(q, accs):
            c8 = c_ref[pl.ds(pl.multiple_of(q * 8, 8), 8), :]
            cs = [jnp.broadcast_to(c8[u : u + 1, :], (8, 128)) for u in range(8)]
            out = []
            for i in range(tiles):
                e = e_ref[
                    pl.ds(pl.multiple_of(base + i * 8, 8), 8),
                    pl.ds(pl.multiple_of(q * 1024, 1024), 1024),
                ]
                p = [e[:, u * 128 : (u + 1) * 128] * cs[u] for u in range(8)]
                while len(p) > 1:
                    p = [p[m] + p[m + 1] for m in range(0, len(p), 2)]
                out.append(accs[i] + p[0])
            return tuple(out)

        zero = jnp.zeros((8, 128), f32)
        accs = lax.fori_loop(0, GROUPS // 8, body, (zero,) * tiles)
        for i in range(tiles):
            acc_ref[pl.ds(pl.multiple_of(base + i * 8, 8), 8), :] = accs[i]

    return rows_to_lanes(acc_ref[...])


def last_row_kernel(c0, c1, c2, c3, z0_ref, z1_ref, e_ref, c_ref, row_ref, kept_ref, acc):
    row = row_pass((c0, c1, c2, c3), e_ref, c_ref, acc)
    row_ref[...] = jnp.concatenate([row, z0_ref[...] + z1_ref[...]], axis=0)


def row_kernel(c0, c1, c2, c3, z_ref, e_ref, c_ref, row_ref, z_out, kept_ref, acc):
    z_out[...] = z_ref[...]
    row = row_pass((c0, c1, c2, c3), e_ref, c_ref, acc)
    row_ref[...] = row


def col_kernel(r0, r1, r2, r3, e_ref, col_ref, kept_ref, rb):
    rb[...] = lanes_to_rows(1.0 / ((r0[...] + r1[...]) + (r2[...] + r3[...])), 128)

    @pl.loop(0, GROUPS // 8)
    def _(q):
        accs = [jnp.zeros((8, 128), f32) for _ in range(8)]
        for i in range(ROWS // 8):
            r = rb[i * 8 : (i + 1) * 8, :]
            e = e_ref[i * 8 : (i + 1) * 8, pl.ds(pl.multiple_of(q * 1024, 1024), 1024)]
            for u in range(8):
                accs[u] = accs[u] + e[:, u * 128 : (u + 1) * 128] * r
        part = jnp.concatenate([jnp.sum(a, axis=0, keepdims=True) for a in accs], axis=0)
        col_ref[pl.ds(pl.multiple_of(q * 8, 8), 8), :] = part


def dz_kernel(rz_ref, c_ref, f_ref, e_ref, p_ref, mine_ref, other_ref, rb, zb, dz_ref):
    step = pl.program_id(0)

    @pl.when(step == 0)
    def _():
        rb[...] = lanes_to_rows(rz_ref[0:1, :], 128)
        zb[...] = lanes_to_rows(rz_ref[1:2, :], 128)
        dz_ref[...] = jnp.zeros_like(dz_ref)

    tall = BLOCK // 128
    cs = c_ref[pl.ds(pl.multiple_of(step * tall, tall), tall), :]
    r = rb[...]
    z = zb[...]
    acc = dz_ref[...]
    for n in range(BLOCK // 256):
        p = p_ref[:, n * 256 : (n + 1) * 256]
        s = jnp.exp2(jnp.dot(f_ref[ROWS:, :], p, preferred_element_type=f32) * KS)
        e = e_ref[:, pl.ds(pl.multiple_of(step * BLOCK + n * 256, 256), 256)]
        parts = []
        for h in range(2):
            lane = slice(h * 128, (h + 1) * 128)
            u = n * 2 + h
            parts.append((s[:, lane] * z - e[:, lane] * r * cs[u : u + 1, :]).astype(bf16))
        g = jnp.concatenate(parts, axis=1)
        acc = acc + lax.dot_general(g, p, (((1,), (1,)), ((), ())), preferred_element_type=f32)
    dz_ref[...] = acc

    @pl.when(step == pl.num_programs(0) - 1)
    def _():
        half = ROWS // 2
        core = lax.axis_index("c")
        mine_ref[...] = dz_ref[pl.ds(pl.multiple_of(core * half, half), half), :]
        other_ref[...] = dz_ref[pl.ds(pl.multiple_of((1 - core) * half, half), half), :]


def pg_kernel(block_ref, r0, r1, r2, r3, c_ref, p_ref, f_ref, out_ref, pt, cb, acc, g, rz):
    step = pl.program_id(0)

    @pl.when(step == 0)
    def _():
        pt[...] = jnp.transpose(p_ref[...].astype(f32)).astype(bf16)
        for q in range(8):
            cb[q * 128 : (q + 1) * 128, :] = lanes_to_rows(c_ref[q : q + 1, :], 128)
        acc[...] = jnp.zeros_like(acc)
        x = lax.axis_index("x")
        y = lax.axis_index("y")
        for dx, ref in enumerate((r0, r1, r2, r3)):
            for dy in range(4):
                rz[lax.rem(x - dx + 4, 4) * 4 + lax.rem(y - dy + 4, 4)] = ref[dy]

    t = f_ref[:, :D]
    s = f_ref[:, D:]
    blocks = range(PG_ROWS // ROWS)
    rzs = [rz[step * len(blocks) + b] for b in blocks]
    r = jnp.concatenate([v[0:1, :] for v in rzs], axis=1)
    z = jnp.concatenate([v[1:2, :] for v in rzs], axis=1)
    nt = (((1,), (1,)), ((), ()))
    for n in range(PG_ROWS // 256):
        rows = slice(n * 256, (n + 1) * 256)
        et = jnp.exp2(lax.dot_general(pt[...], t[rows], nt, preferred_element_type=f32) * KT)
        es = jnp.exp2(lax.dot_general(pt[...], s[rows], nt, preferred_element_type=f32) * KS)
        for h in range(2):
            lane = slice(h * 128, (h + 1) * 128)
            to = slice(n * 256 + h * 128, n * 256 + (h + 1) * 128)
            g[:, to] = (es[:, lane] * z[:, to] - et[:, lane] * r[:, to] * cb[...]).astype(bf16)
    acc[...] += jnp.dot(g[...], s, preferred_element_type=f32)

    @pl.when(step == pl.num_programs(0) - 1)
    def _():
        out_ref[...] = jnp.transpose(acc[...])


def in_vmem(x):
    return pltpu.with_memory_space_constraint(x, pltpu.VMEM)


def in_hbm(x):
    return pltpu.with_memory_space_constraint(x, pltpu.HBM)


def around(x, axis):
    parts = [x]
    for d in (1, 2, 3):
        parts.append(lax.ppermute(x, axis, [(i, (i + d) % 4) for i in range(4)]))
    return parts


def row_terms(rowp):
    pair = pl.pallas_call(
        pair_kernel,
        out_shape=pltpu.VMEM(rowp.shape, f32),
        in_specs=[whole()] * 2,
        out_specs=whole(),
        compiler_params=params(14),
        name="pair",
    )(rowp, lax.ppermute(rowp, "c", [(0, 1), (1, 0)]))
    return around(pair, "z")


def z_call(half, after, feats, protos):
    steps = COLS // 2 // BLOCK
    return pl.pallas_call(
        z_kernel,
        grid=(steps,),
        out_shape=pltpu.VMEM((1, ROWS), f32),
        in_specs=[
            pl.BlockSpec((8, 128), lambda i: (0, 0)),
            whole(),
            pl.BlockSpec((D, BLOCK), lambda i: (0, half * steps + i)),
        ],
        out_specs=whole(),
        scratch_shapes=[pltpu.VMEM((ROWS, 128), f32)],
        compiler_params=params(14),
        name="zden",
    )(after, in_vmem(feats), in_hbm(protos))


def shards(teacher_feats, student_feats, proto_weight):
    core = lax.axis_index("c")
    block = lax.axis_index("x") * 4 + lax.axis_index("y")
    sds = jax.ShapeDtypeStruct
    vmem = pltpu.VMEM
    kept = vmem((ROWS, COLS), f32)

    feats, share = pl.pallas_call(
        norm_kernel,
        grid=(1,),
        out_shape=(vmem((2 * ROWS, D), bf16), sds((SHARE, 2 * D), bf16)),
        in_specs=[pl.BlockSpec((ROWS, D), lambda i: (0, 0))] * 2,
        out_specs=(whole(), whole()),
        compiler_params=params(14),
        name="norm",
    )(in_hbm(teacher_feats), in_hbm(student_feats))
    feats_all = lax.all_gather(share, ALL, axis=0, tiled=True)

    protos, expo, colp = pl.pallas_call(
        first_kernel,
        grid=(COLS // BLOCK,),
        out_shape=(
            pltpu.HBM((D, COLS), bf16),
            kept,
            vmem((GROUPS, 128), f32),
        ),
        in_specs=[pl.BlockSpec((D, BLOCK), lambda i: (0, i)), whole()],
        out_specs=(pl.BlockSpec((D, BLOCK), lambda i: (0, i)), whole(), whole()),
        compiler_params=params(14),
        name="first",
    )(in_hbm(proto_weight), in_vmem(feats))

    for step in range(ITERS):
        parts = around(colp, "y")
        if step == 0:
            z0 = z_call(0, colp, feats, protos)
            colp, z0 = pl.pallas_call(
                sum_z_kernel,
                out_shape=(vmem((GROUPS, 128), f32), vmem((1, ROWS), f32)),
                in_specs=[whole()] * 5,
                out_specs=(whole(), whole()),
                compiler_params=params(14),
                name="sum_z",
            )(*parts, z0)
        else:
            colp = pl.pallas_call(
                sum_kernel,
                out_shape=vmem((GROUPS, 128), f32),
                in_specs=[whole()] * 4,
                out_specs=whole(),
                compiler_params=params(14),
                name="sum",
            )(*parts)
        parts = around(colp, "x")
        if step == 0:
            z1 = z_call(1, colp, feats, protos)
        if step == ITERS - 1:
            break
        unused, rowp, z1, expo = pl.pallas_call(
            row_kernel,
            out_shape=(
                vmem((GROUPS, 128), f32),
                vmem((1, ROWS), f32),
                vmem((1, ROWS), f32),
                kept,
            ),
            in_specs=[whole()] * 6,
            out_specs=(whole(),) * 4,
            input_output_aliases={5: 3},
            scratch_shapes=[vmem((ROWS, 128), f32)],
            compiler_params=params(14),
            name="row",
        )(*parts, in_vmem(z1), in_vmem(expo))
        rowps = row_terms(rowp)
        colp, expo = pl.pallas_call(
            col_kernel,
            out_shape=(vmem((GROUPS, 128), f32), kept),
            in_specs=[whole()] * 5,
            out_specs=(whole(), whole()),
            input_output_aliases={4: 1},
            scratch_shapes=[vmem((ROWS, 128), f32)],
            compiler_params=params(14),
            name="col",
        )(*rowps, in_vmem(expo))

    colsc, rzp, expo = pl.pallas_call(
        last_row_kernel,
        out_shape=(vmem((GROUPS, 128), f32), vmem((2, ROWS), f32), kept),
        in_specs=[whole()] * 7,
        out_specs=(whole(),) * 3,
        input_output_aliases={6: 2},
        scratch_shapes=[vmem((ROWS, 128), f32)],
        compiler_params=params(14),
        name="row_last",
    )(*parts, in_vmem(z0), in_vmem(z1), in_vmem(expo))
    rz = pl.pallas_call(
        rz_kernel,
        out_shape=vmem((2, ROWS), f32),
        in_specs=[whole()] * 4,
        out_specs=whole(),
        compiler_params=params(14),
        name="rz",
    )(*row_terms(rzp))
    rz_y = around(rz, "y")

    half = ROWS // 2
    mine, other = pl.pallas_call(
        dz_kernel,
        grid=(COLS // BLOCK,),
        out_shape=(vmem((half, D), f32), vmem((half, D), f32)),
        in_specs=[whole()] * 4 + [pl.BlockSpec((D, BLOCK), lambda i: (0, i))],
        out_specs=(whole(), whole()),
        scratch_shapes=[vmem((ROWS, 128), f32)] * 2 + [vmem((ROWS, D), f32)],
        compiler_params=params(14),
        name="dz",
    )(in_vmem(rz), in_vmem(colsc), in_vmem(feats), in_vmem(expo), in_hbm(protos))

    rz_rows, other = pl.pallas_call(
        stack_kernel,
        out_shape=(vmem((4, 2, ROWS), f32), vmem((half, D), f32)),
        in_specs=[whole()] * 5,
        out_specs=(whole(), whole()),
        input_output_aliases={4: 1},
        compiler_params=params(14),
        name="stack",
    )(*rz_y, other)
    rz_all = around(rz_rows, "x")

    got = lax.ppermute(other, "c", [(0, 1), (1, 0)])
    parts = around(mine + got, "z")

    proto_grad = pl.pallas_call(
        pg_kernel,
        grid_spec=pltpu.PrefetchScalarGridSpec(
            num_scalar_prefetch=1,
            grid=(NB * ROWS // PG_ROWS,),
            in_specs=[
                *[pl.BlockSpec((4, 2, ROWS), lambda i, b: (0, 0, 0))] * 4,
                pl.BlockSpec((8, 128), lambda i, b: (b[0], 0)),
                pl.BlockSpec((D, OWN), lambda i, b: (0, b[0])),
                pl.BlockSpec((PG_ROWS, 2 * D), lambda i, b: (i, 0)),
            ],
            out_specs=pl.BlockSpec((D, OWN), lambda i, b: (0, 0)),
            scratch_shapes=[
                vmem((OWN, D), bf16),
                vmem((OWN, 128), f32),
                vmem((OWN, D), f32),
                vmem((OWN, PG_ROWS), bf16),
                vmem((NB, 2, ROWS), f32),
            ],
        ),
        out_shape=sds((D, OWN), f32),
        compiler_params=params(14),
        cost_estimate=pl.CostEstimate(flops=9700000000, bytes_accessed=8000000, transcendentals=12600000),
        name="pg",
    )(block.reshape(1), *rz_all, colsc, in_hbm(protos), in_hbm(feats_all))

    parts, proto_grad, student_feats = lax.optimization_barrier(
        (parts, proto_grad, student_feats)
    )
    dz = (parts[0] + parts[2]) + (parts[1] + parts[3])
    feats = lax.dynamic_slice(student_feats, (core * half, 0), (half, D)).astype(f32)
    rnorm = row_norm(feats)
    stud_f = feats * rnorm
    grad = (dz - stud_f * jnp.sum(stud_f * dz, axis=1, keepdims=True)) * rnorm
    sibling = lax.ppermute(grad, "c", [(0, 1), (1, 0)])
    feat_grad = jnp.where(
        core == 0,
        jnp.concatenate([grad, sibling], axis=0),
        jnp.concatenate([sibling, grad], axis=0),
    )
    return (feat_grad, proto_grad)


def solution(mesh):
    grid = Mesh(mesh.devices.reshape(4, 4, 4, 2), ("x", "y", "z", "c"))
    in_specs = (P(XY, None), P(XY, None), P(None, ZC))
    out_specs = (P(XY, None), P(None, ZC + XY))
    return jax.shard_map(shards, mesh=grid, in_specs=in_specs, out_specs=out_specs, check_vma=False)
```

```python
import functools
import math

import jax
import jax.numpy as jnp
from jax import lax
from jax.experimental import pallas as pl
from jax.experimental.pallas import tpu as pltpu
from jax.sharding import Mesh, PartitionSpec as P

D = 256
PROTOS = 131072
ITERS = 3
ROWS = 384
COLS = 16384
OWN = 1024
SHARE = 48
BLOCK = 4096
PG_ROWS = 3072
CHUNK = 2048
KEPT = 2
GROUPS = COLS // 128
NB = 16
KT = math.log2(math.e) / 0.07
KS = math.log2(math.e) / 0.1
GSCALE = PROTOS / 0.1

f32 = jnp.float32
bf16 = jnp.bfloat16
XY = ("x", "y")
ZC = ("z", "c")
ALL = XY + ZC
MIB = 2**20


def whole():
    return pl.BlockSpec(memory_space=pltpu.VMEM)


def params(mib):
    return pltpu.CompilerParams(vmem_limit_bytes=mib * MIB)


def row_norm(feats):
    return lax.rsqrt(jnp.mean(feats * feats, axis=1, keepdims=True) + 1e-06) / math.sqrt(D)


def lanes_to_rows(vec, width):
    return jnp.transpose(jnp.broadcast_to(vec, (width, vec.shape[1])))


def rows_to_lanes(acc):
    return jnp.sum(jnp.transpose(acc), axis=0, keepdims=True)


def norm_kernel(t_ref, s_ref, out_ref, share_ref):
    for src, rows in ((t_ref, slice(0, ROWS)), (s_ref, slice(ROWS, 2 * ROWS))):
        feats = src[...].astype(f32)
        out_ref[rows, :] = (feats * row_norm(feats)).astype(bf16)
    start = (lax.axis_index("z") * 2 + lax.axis_index("c")) * SHARE
    for k in range(2):
        rows = pl.ds(pl.multiple_of(k * ROWS + start, SHARE), SHARE)
        share_ref[:, k * D : (k + 1) * D] = out_ref[rows, :]


def first_kernel(w_ref, f_ref, p_ref, e_ref, col_ref, sems):
    count = COLS // CHUNK

    def fetch(k):
        lanes = pl.ds(pl.multiple_of(k * CHUNK, CHUNK), CHUNK)
        return pltpu.make_async_copy(w_ref.at[:, lanes], p_ref.at[k], sems.at[k])

    for k in range(count):
        fetch(k).start()

    @pl.loop(0, count)
    def _(k):
        fetch(k).wait()
        sums = []
        for n in range(CHUNK // 256):
            lanes = slice(n * 256, (n + 1) * 256)
            w = p_ref[k, :, lanes].astype(f32)
            inv = lax.rsqrt(jnp.mean(w * w, axis=0, keepdims=True) + 1e-06) / math.sqrt(D)
            p = (w * inv).astype(bf16)
            p_ref[k, :, lanes] = p
            e = jnp.exp2(jnp.dot(f_ref[:ROWS, :], p, preferred_element_type=f32) * KT)
            e_ref[:, pl.ds(pl.multiple_of(k * CHUNK + n * 256, 256), 256)] = e
            for h in range(2):
                sums.append(jnp.sum(e[:, h * 128 : (h + 1) * 128], axis=0, keepdims=True))
        tall = CHUNK // 128
        col_ref[pl.ds(pl.multiple_of(k * tall, tall), tall), :] = jnp.concatenate(sums, axis=0)


def z_kernel(half, after_ref, f_ref, p_ref, z_ref):
    pairs = COLS // CHUNK // 4

    def body(k, zsum):
        for m in range(2):
            chunk = (half * pairs + k) * 2 + m
            for n in range(CHUNK // 256):
                p = p_ref[chunk, :, n * 256 : (n + 1) * 256]
                s = jnp.exp2(jnp.dot(f_ref[ROWS:, :], p, preferred_element_type=f32) * KS)
                zsum = zsum + s[:, :128] + s[:, 128:]
        return zsum

    z_ref[...] = rows_to_lanes(lax.fori_loop(0, pairs, body, jnp.zeros((ROWS, 128), f32)))


def sum_kernel(a_ref, b_ref, c_ref, d_ref, out_ref):
    out_ref[...] = (a_ref[...] + b_ref[...]) + (c_ref[...] + d_ref[...])


def pair_kernel(a_ref, b_ref, out_ref):
    out_ref[...] = a_ref[...] + b_ref[...]


def prep_kernel(after_ref, c_ref, p_ref, pt_ref, cb_ref, done_ref):
    x = lax.axis_index("x")
    y = lax.axis_index("y")
    lanes = pl.ds(pl.multiple_of(lax.rem(y, 2) * OWN, OWN), OWN)
    pt_ref[...] = jnp.transpose(p_ref[x * 2 + lax.div(y, 2), :, lanes].astype(f32)).astype(bf16)
    own = c_ref[pl.ds(pl.multiple_of((x * 4 + y) * 8, 8), 8), :]
    for q in range(8):
        cb_ref[q * 128 : (q + 1) * 128, :] = lanes_to_rows(own[q : q + 1, :], 128)
    done_ref[...] = jnp.zeros_like(done_ref)


def rz_kernel(a_ref, b_ref, c_ref, d_ref, after_ref, out_ref):
    out_ref[...] = GSCALE / ((a_ref[...] + b_ref[...]) + (c_ref[...] + d_ref[...]))


def stack_kernel(a_ref, b_ref, c_ref, d_ref, other_ref, out_ref, kept_ref):
    for d, ref in enumerate((a_ref, b_ref, c_ref, d_ref)):
        out_ref[d] = ref[...]


def sum_z_kernel(a_ref, b_ref, c_ref, d_ref, z_ref, out_ref, z_out):
    out_ref[...] = (a_ref[...] + b_ref[...]) + (c_ref[...] + d_ref[...])
    z_out[...] = z_ref[...]


def row_pass(cols, e_ref, c_ref, acc_ref):
    c_ref[...] = 1.0 / ((cols[0][...] + cols[1][...]) + (cols[2][...] + cols[3][...]))
    tiles = 12

    @pl.loop(0, ROWS // (8 * tiles))
    def _(k):
        base = pl.multiple_of(k * 8 * tiles, 8 * tiles)

        def body(q, accs):
            c8 = c_ref[pl.ds(pl.multiple_of(q * 8, 8), 8), :]
            cs = [jnp.broadcast_to(c8[u : u + 1, :], (8, 128)) for u in range(8)]
            out = []
            for i in range(tiles):
                e = e_ref[
                    pl.ds(pl.multiple_of(base + i * 8, 8), 8),
                    pl.ds(pl.multiple_of(q * 1024, 1024), 1024),
                ]
                p = [e[:, u * 128 : (u + 1) * 128] * cs[u] for u in range(8)]
                while len(p) > 1:
                    p = [p[m] + p[m + 1] for m in range(0, len(p), 2)]
                out.append(accs[i] + p[0])
            return tuple(out)

        zero = jnp.zeros((8, 128), f32)
        accs = lax.fori_loop(0, GROUPS // 8, body, (zero,) * tiles)
        for i in range(tiles):
            acc_ref[pl.ds(pl.multiple_of(base + i * 8, 8), 8), :] = accs[i]

    return rows_to_lanes(acc_ref[...])


def last_row_kernel(c0, c1, c2, c3, z0_ref, z1_ref, *refs):
    e_ref, (c_ref, row_ref), acc = refs[0], refs[KEPT : KEPT + 2], refs[-1]
    row = row_pass((c0, c1, c2, c3), e_ref, c_ref, acc)
    row_ref[...] = jnp.concatenate([row, z0_ref[...] + z1_ref[...]], axis=0)


def row_kernel(c0, c1, c2, c3, *refs):
    e_ref, (c_ref, row_ref), acc = refs[0], refs[KEPT : KEPT + 2], refs[-1]
    row_ref[...] = row_pass((c0, c1, c2, c3), e_ref, c_ref, acc)


def row_z_kernel(c0, c1, c2, c3, z_ref, *refs):
    e_ref, (c_ref, row_ref, z_out), acc = refs[0], refs[KEPT : KEPT + 3], refs[-1]
    row_ref[...] = row_pass((c0, c1, c2, c3), e_ref, c_ref, acc)
    z_out[...] = z_ref[...]


def col_kernel(r0, r1, r2, r3, *refs):
    e_ref, col_ref, rb = refs[0], refs[len(refs) // 2 - 1], refs[-1]
    rb[...] = lanes_to_rows(1.0 / ((r0[...] + r1[...]) + (r2[...] + r3[...])), 128)

    @pl.loop(0, GROUPS // 8)
    def _(q):
        accs = [jnp.zeros((8, 128), f32) for _ in range(8)]
        for i in range(ROWS // 8):
            r = rb[i * 8 : (i + 1) * 8, :]
            e = e_ref[i * 8 : (i + 1) * 8, pl.ds(pl.multiple_of(q * 1024, 1024), 1024)]
            for u in range(8):
                accs[u] = accs[u] + e[:, u * 128 : (u + 1) * 128] * r
        part = jnp.concatenate([jnp.sum(a, axis=0, keepdims=True) for a in accs], axis=0)
        col_ref[pl.ds(pl.multiple_of(q * 8, 8), 8), :] = part


def dz_kernel(rz_ref, c_ref, f_ref, e_ref, p_ref, mine_ref, other_ref, rb, zb, dz_ref):
    rb[...] = lanes_to_rows(rz_ref[0:1, :], 128)
    zb[...] = lanes_to_rows(rz_ref[1:2, :], 128)
    dz_ref[...] = jnp.zeros_like(dz_ref)
    tall = BLOCK // 128

    @pl.loop(0, COLS // BLOCK)
    def _(k):
        cs = c_ref[pl.ds(pl.multiple_of(k * tall, tall), tall), :]
        r = rb[...]
        z = zb[...]
        acc = dz_ref[...]
        for n in range(BLOCK // 256):
            m, at = divmod(n * 256, CHUNK)
            p = p_ref[k * (BLOCK // CHUNK) + m, :, at : at + 256]
            s = jnp.exp2(jnp.dot(f_ref[ROWS:, :], p, preferred_element_type=f32) * KS)
            e = e_ref[:, pl.ds(pl.multiple_of(k * BLOCK + n * 256, 256), 256)]
            parts = []
            for h in range(2):
                lane = slice(h * 128, (h + 1) * 128)
                u = n * 2 + h
                parts.append((s[:, lane] * z - e[:, lane] * r * cs[u : u + 1, :]).astype(bf16))
            g = jnp.concatenate(parts, axis=1)
            acc = acc + lax.dot_general(
                g, p, (((1,), (1,)), ((), ())), preferred_element_type=f32
            )
        dz_ref[...] = acc

    half = ROWS // 2
    core = lax.axis_index("c")
    mine_ref[...] = dz_ref[pl.ds(pl.multiple_of(core * half, half), half), :]
    other_ref[...] = dz_ref[pl.ds(pl.multiple_of((1 - core) * half, half), half), :]


def pg_kernel(r0, r1, r2, r3, pt, cb, f_ref, out_ref, acc, g, rz):
    step = pl.program_id(0)

    @pl.when(step == 0)
    def _():
        acc[...] = jnp.zeros_like(acc)
        x = lax.axis_index("x")
        y = lax.axis_index("y")
        for dx, ref in enumerate((r0, r1, r2, r3)):
            for dy in range(4):
                rz[lax.rem(x - dx + 4, 4) * 4 + lax.rem(y - dy + 4, 4)] = ref[dy]

    t = f_ref[:, :D]
    s = f_ref[:, D:]
    blocks = range(PG_ROWS // ROWS)
    rzs = [rz[step * len(blocks) + b] for b in blocks]
    r = jnp.concatenate([v[0:1, :] for v in rzs], axis=1)
    z = jnp.concatenate([v[1:2, :] for v in rzs], axis=1)
    nt = (((1,), (1,)), ((), ()))
    for n in range(PG_ROWS // 256):
        rows = slice(n * 256, (n + 1) * 256)
        et = jnp.exp2(lax.dot_general(pt[...], t[rows], nt, preferred_element_type=f32) * KT)
        es = jnp.exp2(lax.dot_general(pt[...], s[rows], nt, preferred_element_type=f32) * KS)
        for h in range(2):
            lane = slice(h * 128, (h + 1) * 128)
            to = slice(n * 256 + h * 128, n * 256 + (h + 1) * 128)
            g[:, to] = (es[:, lane] * z[:, to] - et[:, lane] * r[:, to] * cb[...]).astype(bf16)
    acc[...] += jnp.dot(g[...], s, preferred_element_type=f32)

    @pl.when(step == pl.num_programs(0) - 1)
    def _():
        out_ref[...] = jnp.transpose(acc[...])


def in_vmem(x):
    return pltpu.with_memory_space_constraint(x, pltpu.VMEM)


def in_hbm(x):
    return pltpu.with_memory_space_constraint(x, pltpu.HBM)


def around(x, axis):
    parts = [x]
    for d in (1, 2, 3):
        parts.append(lax.ppermute(x, axis, [(i, (i + d) % 4) for i in range(4)]))
    return parts


def row_terms(rowp):
    pair = pl.pallas_call(
        pair_kernel,
        out_shape=pltpu.VMEM(rowp.shape, f32),
        in_specs=[whole()] * 2,
        out_specs=whole(),
        compiler_params=params(5),
        name="pair",
    )(rowp, lax.ppermute(rowp, "c", [(0, 1), (1, 0)]))
    return around(pair, "z")


def z_call(half, after, feats, protos):
    return pl.pallas_call(
        functools.partial(z_kernel, half),
        out_shape=pltpu.VMEM((1, ROWS), f32),
        in_specs=[whole()] * 3,
        out_specs=whole(),
        compiler_params=params(5),
        name="zden",
    )(after, in_vmem(feats), in_vmem(protos))


def shards(teacher_feats, student_feats, proto_weight):
    core = lax.axis_index("c")
    sds = jax.ShapeDtypeStruct
    vmem = pltpu.VMEM
    kept = vmem((ROWS, COLS), f32)

    feats, share = pl.pallas_call(
        norm_kernel,
        grid=(1,),
        out_shape=(vmem((2 * ROWS, D), bf16), sds((SHARE, 2 * D), bf16)),
        in_specs=[pl.BlockSpec((ROWS, D), lambda i: (0, 0))] * 2,
        out_specs=(whole(), whole()),
        compiler_params=params(5),
        name="norm",
    )(in_hbm(teacher_feats), in_hbm(student_feats))
    feats_all = lax.all_gather(share, ALL, axis=0, tiled=True)

    packed = vmem((COLS // CHUNK, D, CHUNK), bf16)
    protos, expo, colp = pl.pallas_call(
        first_kernel,
        out_shape=(packed, kept, vmem((GROUPS, 128), f32)),
        in_specs=[pl.BlockSpec(memory_space=pl.ANY), whole()],
        out_specs=(whole(), whole(), whole()),
        scratch_shapes=[pltpu.SemaphoreType.DMA((COLS // CHUNK,))],
        compiler_params=params(5),
        name="first",
    )(in_hbm(proto_weight), in_vmem(feats))

    keep = [expo, protos]
    shapes = [kept, packed]
    for step in range(ITERS):
        parts = around(colp, "y")
        if step == 2:
            z1 = z_call(1, colp, feats, keep[1])
            colp, z1 = pl.pallas_call(
                sum_z_kernel,
                out_shape=(vmem((GROUPS, 128), f32), vmem((1, ROWS), f32)),
                in_specs=[whole()] * 5,
                out_specs=(whole(), whole()),
                compiler_params=params(5),
                name="sum_z",
            )(*parts, z1)
        else:
            colp = pl.pallas_call(
                sum_kernel,
                out_shape=vmem((GROUPS, 128), f32),
                in_specs=[whole()] * 4,
                out_specs=whole(),
                compiler_params=params(5),
                name="sum",
            )(*parts)
        parts = around(colp, "x")
        if step == 2:
            break
        if step == 0:
            unused, rowp, *keep = pl.pallas_call(
                row_kernel,
                out_shape=[vmem((GROUPS, 128), f32), vmem((1, ROWS), f32)] + shapes,
                in_specs=[whole()] * (4 + KEPT),
                out_specs=[whole()] * (2 + KEPT),
                input_output_aliases={4 + k: 2 + k for k in range(KEPT)},
                scratch_shapes=[vmem((ROWS, 128), f32)],
                compiler_params=params(5),
                name="row",
            )(*parts, *map(in_vmem, keep))
        else:
            z0 = z_call(0, colp, feats, keep[1])
            unused, rowp, z0, *keep = pl.pallas_call(
                row_z_kernel,
                out_shape=[vmem((GROUPS, 128), f32), vmem((1, ROWS), f32), vmem((1, ROWS), f32)]
                + shapes,
                in_specs=[whole()] * (5 + KEPT),
                out_specs=[whole()] * (3 + KEPT),
                input_output_aliases={5 + k: 3 + k for k in range(KEPT)},
                scratch_shapes=[vmem((ROWS, 128), f32)],
                compiler_params=params(5),
                name="row",
            )(*parts, in_vmem(z0), *map(in_vmem, keep))
        rowps = row_terms(rowp)
        colp, *keep = pl.pallas_call(
            col_kernel,
            out_shape=[vmem((GROUPS, 128), f32)] + shapes,
            in_specs=[whole()] * (4 + len(keep)),
            out_specs=[whole()] * (1 + len(keep)),
            input_output_aliases={4 + k: 1 + k for k in range(len(keep))},
            scratch_shapes=[vmem((ROWS, 128), f32)],
            compiler_params=params(5),
            name="col",
        )(*rowps, *map(in_vmem, keep))

    colsc, rzp, *keep = pl.pallas_call(
        last_row_kernel,
        out_shape=[vmem((GROUPS, 128), f32), vmem((2, ROWS), f32)] + shapes,
        in_specs=[whole()] * (6 + KEPT),
        out_specs=[whole()] * (2 + KEPT),
        input_output_aliases={6 + k: 2 + k for k in range(KEPT)},
        scratch_shapes=[vmem((ROWS, 128), f32)],
        compiler_params=params(5),
        name="row_last",
    )(*parts, in_vmem(z0), in_vmem(z1), *map(in_vmem, keep))
    terms = row_terms(rzp)
    pt, cb, token = pl.pallas_call(
        prep_kernel,
        out_shape=(vmem((OWN, D), bf16), vmem((OWN, 128), f32), vmem((8, 128), f32)),
        in_specs=[whole()] * 3,
        out_specs=(whole(),) * 3,
        compiler_params=params(5),
        name="prep",
    )(terms[0], in_vmem(colsc), in_vmem(keep[1]))
    rz = pl.pallas_call(
        rz_kernel,
        out_shape=vmem((2, ROWS), f32),
        in_specs=[whole()] * 5,
        out_specs=whole(),
        compiler_params=params(5),
        name="rz",
    )(*terms, token)
    rz_y = around(rz, "y")

    half = ROWS // 2
    mine, other = pl.pallas_call(
        dz_kernel,
        out_shape=(vmem((half, D), f32), vmem((half, D), f32)),
        in_specs=[whole()] * 5,
        out_specs=(whole(), whole()),
        scratch_shapes=[vmem((ROWS, 128), f32)] * 2 + [vmem((ROWS, D), f32)],
        compiler_params=params(5),
        name="dz",
    )(in_vmem(rz), in_vmem(colsc), in_vmem(feats), *map(in_vmem, keep))

    rz_rows, other = pl.pallas_call(
        stack_kernel,
        out_shape=(vmem((4, 2, ROWS), f32), vmem((half, D), f32)),
        in_specs=[whole()] * 5,
        out_specs=(whole(), whole()),
        input_output_aliases={4: 1},
        compiler_params=params(5),
        name="stack",
    )(*rz_y, other)
    rz_all = around(rz_rows, "x")

    got = lax.ppermute(other, "c", [(0, 1), (1, 0)])
    parts = around(mine + got, "z")

    proto_grad = pl.pallas_call(
        pg_kernel,
        grid=(NB * ROWS // PG_ROWS,),
        out_shape=sds((D, OWN), f32),
        in_specs=[whole()] * 6 + [pl.BlockSpec((PG_ROWS, 2 * D), lambda i: (i, 0))],
        out_specs=pl.BlockSpec((D, OWN), lambda i: (0, 0)),
        scratch_shapes=[
            vmem((OWN, D), f32),
            vmem((OWN, PG_ROWS), bf16),
            vmem((NB, 2, ROWS), f32),
        ],
        compiler_params=params(30),
        cost_estimate=pl.CostEstimate(flops=9700000000, bytes_accessed=8000000, transcendentals=12600000),
        name="pg",
    )(*rz_all, in_vmem(pt), in_vmem(cb), in_hbm(feats_all))

    parts, proto_grad, student_feats = lax.optimization_barrier(
        (parts, proto_grad, student_feats)
    )
    dz = (parts[0] + parts[2]) + (parts[1] + parts[3])
    feats = lax.dynamic_slice(student_feats, (core * half, 0), (half, D)).astype(f32)
    rnorm = row_norm(feats)
    stud_f = feats * rnorm
    grad = (dz - stud_f * jnp.sum(stud_f * dz, axis=1, keepdims=True)) * rnorm
    sibling = lax.ppermute(grad, "c", [(0, 1), (1, 0)])
    feat_grad = jnp.where(
        core == 0,
        jnp.concatenate([grad, sibling], axis=0),
        jnp.concatenate([sibling, grad], axis=0),
    )
    return (feat_grad, proto_grad)


def solution(mesh):
    grid = Mesh(mesh.devices.reshape(4, 4, 4, 2), ("x", "y", "z", "c"))
    in_specs = (P(XY, None), P(XY, None), P(None, ZC))
    out_specs = (P(XY, None), P(None, ZC + XY))
    return jax.shard_map(shards, mesh=grid, in_specs=in_specs, out_specs=out_specs, check_vma=False)
```

```python
import functools
import math

import jax
import jax.numpy as jnp
from jax import lax
from jax.experimental import pallas as pl
from jax.experimental.pallas import tpu as pltpu
from jax.sharding import Mesh, PartitionSpec as P

D = 256
PROTOS = 131072
ITERS = 3
ROWS = 384
COLS = 16384
OWN = 1024
SHARE = 48
BLOCK = 8192
PG_ROWS = 3072
CHUNK = 2048
KEPT = 2
GROUPS = COLS // 128
NB = 16
KT = math.log2(math.e) / 0.07
KS = math.log2(math.e) / 0.1
GSCALE = PROTOS / 0.1

f32 = jnp.float32
bf16 = jnp.bfloat16
XY = ("x", "y")
ZC = ("z", "c")
ALL = XY + ZC
MIB = 2**20


def whole():
    return pl.BlockSpec(memory_space=pltpu.VMEM)


def params(mib):
    return pltpu.CompilerParams(vmem_limit_bytes=mib * MIB)


def row_norm(feats):
    return lax.rsqrt(jnp.mean(feats * feats, axis=1, keepdims=True) + 1e-06) / math.sqrt(D)


def lanes_to_rows(vec, width):
    return jnp.transpose(jnp.broadcast_to(vec, (width, vec.shape[1])))


def rows_to_lanes(acc):
    return jnp.sum(jnp.transpose(acc), axis=0, keepdims=True)


def norm_kernel(t_ref, s_ref, out_ref, share_ref):
    for src, rows in ((t_ref, slice(0, ROWS)), (s_ref, slice(ROWS, 2 * ROWS))):
        feats = src[...].astype(f32)
        out_ref[rows, :] = (feats * row_norm(feats)).astype(bf16)
    start = (lax.axis_index("z") * 2 + lax.axis_index("c")) * SHARE
    for k in range(2):
        rows = pl.ds(pl.multiple_of(k * ROWS + start, SHARE), SHARE)
        share_ref[:, k * D : (k + 1) * D] = out_ref[rows, :]


def first_kernel(w_ref, f_ref, p_ref, e_ref, col_ref, sems):
    count = COLS // CHUNK

    def fetch(k):
        lanes = pl.ds(pl.multiple_of(k * CHUNK, CHUNK), CHUNK)
        return pltpu.make_async_copy(w_ref.at[:, lanes], p_ref.at[k], sems.at[k])

    for k in range(count):
        fetch(k).start()

    @pl.loop(0, count)
    def _(k):
        fetch(k).wait()
        sums = []
        for n in range(CHUNK // 256):
            lanes = slice(n * 256, (n + 1) * 256)
            w = p_ref[k, :, lanes].astype(f32)
            inv = lax.rsqrt(jnp.mean(w * w, axis=0, keepdims=True) + 1e-06) / math.sqrt(D)
            p = (w * inv).astype(bf16)
            p_ref[k, :, lanes] = p
            e = jnp.exp2(jnp.dot(f_ref[:ROWS, :], p, preferred_element_type=f32) * KT)
            e_ref[:, pl.ds(pl.multiple_of(k * CHUNK + n * 256, 256), 256)] = e
            for h in range(2):
                sums.append(jnp.sum(e[:, h * 128 : (h + 1) * 128], axis=0, keepdims=True))
        tall = CHUNK // 128
        col_ref[pl.ds(pl.multiple_of(k * tall, tall), tall), :] = jnp.concatenate(sums, axis=0)


def z_kernel(half, after_ref, f_ref, p_ref, z_ref):
    pairs = COLS // CHUNK // 4

    def body(k, zsum):
        for m in range(2):
            chunk = (half * pairs + k) * 2 + m
            for n in range(CHUNK // 256):
                p = p_ref[chunk, :, n * 256 : (n + 1) * 256]
                s = jnp.exp2(jnp.dot(f_ref[ROWS:, :], p, preferred_element_type=f32) * KS)
                zsum = zsum + s[:, :128] + s[:, 128:]
        return zsum

    z_ref[...] = rows_to_lanes(lax.fori_loop(0, pairs, body, jnp.zeros((ROWS, 128), f32)))


def sum_kernel(a_ref, b_ref, c_ref, d_ref, out_ref):
    out_ref[...] = (a_ref[...] + b_ref[...]) + (c_ref[...] + d_ref[...])


def pair_kernel(a_ref, b_ref, out_ref):
    out_ref[...] = a_ref[...] + b_ref[...]


def prep_kernel(after_ref, c_ref, p_ref, pt_ref, cb_ref, done_ref):
    x = lax.axis_index("x")
    y = lax.axis_index("y")
    block, per = x * 4 + y, CHUNK // OWN
    lanes = pl.ds(pl.multiple_of(lax.rem(block, per) * OWN, OWN), OWN)
    pt_ref[...] = jnp.transpose(p_ref[lax.div(block, per), :, lanes].astype(f32)).astype(bf16)
    own = c_ref[pl.ds(pl.multiple_of(block * 8, 8), 8), :]
    for q in range(8):
        cb_ref[q * 128 : (q + 1) * 128, :] = lanes_to_rows(own[q : q + 1, :], 128)
    done_ref[...] = jnp.zeros_like(done_ref)


def rz_kernel(a_ref, b_ref, c_ref, d_ref, after_ref, out_ref):
    out_ref[...] = GSCALE / ((a_ref[...] + b_ref[...]) + (c_ref[...] + d_ref[...]))


def stack_kernel(a_ref, b_ref, c_ref, d_ref, other_ref, out_ref, kept_ref):
    for d, ref in enumerate((a_ref, b_ref, c_ref, d_ref)):
        out_ref[d] = ref[...]


def sum_z_kernel(a_ref, b_ref, c_ref, d_ref, z_ref, out_ref, z_out):
    out_ref[...] = (a_ref[...] + b_ref[...]) + (c_ref[...] + d_ref[...])
    z_out[...] = z_ref[...]


def row_pass(cols, e_ref, c_ref, acc_ref):
    c_ref[...] = 1.0 / ((cols[0][...] + cols[1][...]) + (cols[2][...] + cols[3][...]))
    tiles = 12

    @pl.loop(0, ROWS // (8 * tiles))
    def _(k):
        base = pl.multiple_of(k * 8 * tiles, 8 * tiles)

        def body(q, accs):
            c8 = c_ref[pl.ds(pl.multiple_of(q * 8, 8), 8), :]
            cs = [jnp.broadcast_to(c8[u : u + 1, :], (8, 128)) for u in range(8)]
            out = []
            for i in range(tiles):
                e = e_ref[
                    pl.ds(pl.multiple_of(base + i * 8, 8), 8),
                    pl.ds(pl.multiple_of(q * 1024, 1024), 1024),
                ]
                p = [e[:, u * 128 : (u + 1) * 128] * cs[u] for u in range(8)]
                while len(p) > 1:
                    p = [p[m] + p[m + 1] for m in range(0, len(p), 2)]
                out.append(accs[i] + p[0])
            return tuple(out)

        zero = jnp.zeros((8, 128), f32)
        accs = lax.fori_loop(0, GROUPS // 8, body, (zero,) * tiles)
        for i in range(tiles):
            acc_ref[pl.ds(pl.multiple_of(base + i * 8, 8), 8), :] = accs[i]

    return rows_to_lanes(acc_ref[...])


def last_row_kernel(c0, c1, c2, c3, z0_ref, z1_ref, *refs):
    e_ref, (c_ref, row_ref), acc = refs[0], refs[KEPT : KEPT + 2], refs[-1]
    row = row_pass((c0, c1, c2, c3), e_ref, c_ref, acc)
    row_ref[...] = jnp.concatenate([row, z0_ref[...] + z1_ref[...]], axis=0)


def row_kernel(c0, c1, c2, c3, *refs):
    e_ref, row_ref, (c_ref, acc) = refs[0], refs[KEPT], refs[-2:]
    row_ref[...] = row_pass((c0, c1, c2, c3), e_ref, c_ref, acc)


def row_z_kernel(c0, c1, c2, c3, z_ref, *refs):
    e_ref, (row_ref, z_out), (c_ref, acc) = refs[0], refs[KEPT : KEPT + 2], refs[-2:]
    row_ref[...] = row_pass((c0, c1, c2, c3), e_ref, c_ref, acc)
    z_out[...] = z_ref[...]


def col_kernel(r0, r1, r2, r3, *refs):
    e_ref, col_ref, rb = refs[0], refs[len(refs) // 2 - 1], refs[-1]
    rb[...] = lanes_to_rows(1.0 / ((r0[...] + r1[...]) + (r2[...] + r3[...])), 128)

    @pl.loop(0, GROUPS // 8)
    def _(q):
        accs = [jnp.zeros((8, 128), f32) for _ in range(8)]
        for i in range(ROWS // 8):
            r = rb[i * 8 : (i + 1) * 8, :]
            e = e_ref[i * 8 : (i + 1) * 8, pl.ds(pl.multiple_of(q * 1024, 1024), 1024)]
            for u in range(8):
                accs[u] = accs[u] + e[:, u * 128 : (u + 1) * 128] * r
        part = jnp.concatenate([jnp.sum(a, axis=0, keepdims=True) for a in accs], axis=0)
        col_ref[pl.ds(pl.multiple_of(q * 8, 8), 8), :] = part


def dz_kernel(rz_ref, c_ref, f_ref, e_ref, p_ref, mine_ref, other_ref, rb, zb, dz_ref):
    rb[...] = lanes_to_rows(rz_ref[0:1, :], 128)
    zb[...] = lanes_to_rows(rz_ref[1:2, :], 128)
    dz_ref[...] = jnp.zeros_like(dz_ref)
    tall = BLOCK // 128

    @pl.loop(0, COLS // BLOCK)
    def _(k):
        cs = c_ref[pl.ds(pl.multiple_of(k * tall, tall), tall), :]
        r = rb[...]
        z = zb[...]
        acc = dz_ref[...]
        for n in range(BLOCK // 256):
            m, at = divmod(n * 256, CHUNK)
            p = p_ref[k * (BLOCK // CHUNK) + m, :, at : at + 256]
            s = jnp.exp2(jnp.dot(f_ref[ROWS:, :], p, preferred_element_type=f32) * KS)
            e = e_ref[:, pl.ds(pl.multiple_of(k * BLOCK + n * 256, 256), 256)]
            parts = []
            for h in range(2):
                lane = slice(h * 128, (h + 1) * 128)
                u = n * 2 + h
                parts.append((s[:, lane] * z - e[:, lane] * r * cs[u : u + 1, :]).astype(bf16))
            g = jnp.concatenate(parts, axis=1)
            acc = acc + lax.dot_general(
                g, p, (((1,), (1,)), ((), ())), preferred_element_type=f32
            )
        dz_ref[...] = acc

    half = ROWS // 2
    core = lax.axis_index("c")
    mine_ref[...] = dz_ref[pl.ds(pl.multiple_of(core * half, half), half), :]
    other_ref[...] = dz_ref[pl.ds(pl.multiple_of((1 - core) * half, half), half), :]


def pg_kernel(r0, r1, r2, r3, pt, cb, f_ref, out_ref, acc, g, rz):
    step = pl.program_id(0)

    @pl.when(step == 0)
    def _():
        acc[...] = jnp.zeros_like(acc)
        x = lax.axis_index("x")
        y = lax.axis_index("y")
        for dx, ref in enumerate((r0, r1, r2, r3)):
            for dy in range(4):
                rz[lax.rem(x - dx + 4, 4) * 4 + lax.rem(y - dy + 4, 4)] = ref[dy]

    t = f_ref[:, :D]
    s = f_ref[:, D:]
    blocks = range(PG_ROWS // ROWS)
    rzs = [rz[step * len(blocks) + b] for b in blocks]
    r = jnp.concatenate([v[0:1, :] for v in rzs], axis=1)
    z = jnp.concatenate([v[1:2, :] for v in rzs], axis=1)
    nt = (((1,), (1,)), ((), ()))
    for n in range(PG_ROWS // 256):
        rows = slice(n * 256, (n + 1) * 256)
        et = jnp.exp2(lax.dot_general(pt[...], t[rows], nt, preferred_element_type=f32) * KT)
        es = jnp.exp2(lax.dot_general(pt[...], s[rows], nt, preferred_element_type=f32) * KS)
        for h in range(2):
            lane = slice(h * 128, (h + 1) * 128)
            to = slice(n * 256 + h * 128, n * 256 + (h + 1) * 128)
            g[:, to] = (es[:, lane] * z[:, to] - et[:, lane] * r[:, to] * cb[...]).astype(bf16)
    acc[...] += jnp.dot(g[...], s, preferred_element_type=f32)

    @pl.when(step == pl.num_programs(0) - 1)
    def _():
        out_ref[...] = jnp.transpose(acc[...])


def end_kernel(a_ref, b_ref, c_ref, d_ref, s_ref, out_ref):
    half = ROWS // 2
    start = lax.axis_index("c") * half
    feats = s_ref[pl.ds(pl.multiple_of(start, half), half), :].astype(f32)
    rnorm = row_norm(feats)
    stud_f = feats * rnorm
    dz = (a_ref[...] + c_ref[...]) + (b_ref[...] + d_ref[...])
    out_ref[...] = (dz - stud_f * jnp.sum(stud_f * dz, axis=1, keepdims=True)) * rnorm


def place_kernel(own_ref, sibling_ref, out_ref):
    half = ROWS // 2
    core = lax.axis_index("c")
    out_ref[pl.ds(pl.multiple_of(core * half, half), half), :] = own_ref[...]
    out_ref[pl.ds(pl.multiple_of((1 - core) * half, half), half), :] = sibling_ref[...]


def in_vmem(x):
    return pltpu.with_memory_space_constraint(x, pltpu.VMEM)


def in_hbm(x):
    return pltpu.with_memory_space_constraint(x, pltpu.HBM)


def around(x, axis):
    parts = [x]
    for d in (1, 2, 3):
        parts.append(lax.ppermute(x, axis, [(i, (i + d) % 4) for i in range(4)]))
    return parts


def row_terms(rowp):
    pair = pl.pallas_call(
        pair_kernel,
        out_shape=pltpu.VMEM(rowp.shape, f32),
        in_specs=[whole()] * 2,
        out_specs=whole(),
        compiler_params=params(5),
        name="pair",
    )(rowp, lax.ppermute(rowp, "c", [(0, 1), (1, 0)]))
    return around(pair, "z")


def z_call(half, after, feats, protos):
    return pl.pallas_call(
        functools.partial(z_kernel, half),
        out_shape=pltpu.VMEM((1, ROWS), f32),
        in_specs=[whole()] * 3,
        out_specs=whole(),
        compiler_params=params(5),
        name="zden",
    )(after, in_vmem(feats), in_vmem(protos))


def shards(teacher_feats, student_feats, proto_weight):
    sds = jax.ShapeDtypeStruct
    vmem = pltpu.VMEM
    kept = vmem((ROWS, COLS), f32)

    feats, share = pl.pallas_call(
        norm_kernel,
        grid=(1,),
        out_shape=(vmem((2 * ROWS, D), bf16), sds((SHARE, 2 * D), bf16)),
        in_specs=[pl.BlockSpec((ROWS, D), lambda i: (0, 0))] * 2,
        out_specs=(whole(), whole()),
        compiler_params=params(5),
        name="norm",
    )(in_hbm(teacher_feats), in_hbm(student_feats))
    feats_all = lax.all_gather(share, ALL, axis=0, tiled=True)

    packed = vmem((COLS // CHUNK, D, CHUNK), bf16)
    protos, expo, colp = pl.pallas_call(
        first_kernel,
        out_shape=(packed, kept, vmem((GROUPS, 128), f32)),
        in_specs=[pl.BlockSpec(memory_space=pl.ANY), whole()],
        out_specs=(whole(), whole(), whole()),
        scratch_shapes=[pltpu.SemaphoreType.DMA((COLS // CHUNK,))],
        compiler_params=params(5),
        name="first",
    )(in_hbm(proto_weight), in_vmem(feats))

    keep = [expo, protos]
    shapes = [kept, packed]
    for step in range(ITERS):
        parts = around(colp, "y")
        if step == 2:
            z1 = z_call(1, colp, feats, keep[1])
            colp, z1 = pl.pallas_call(
                sum_z_kernel,
                out_shape=(vmem((GROUPS, 128), f32), vmem((1, ROWS), f32)),
                in_specs=[whole()] * 5,
                out_specs=(whole(), whole()),
                compiler_params=params(5),
                name="sum_z",
            )(*parts, z1)
        else:
            colp = pl.pallas_call(
                sum_kernel,
                out_shape=vmem((GROUPS, 128), f32),
                in_specs=[whole()] * 4,
                out_specs=whole(),
                compiler_params=params(5),
                name="sum",
            )(*parts)
        parts = around(colp, "x")
        if step == 2:
            break
        if step == 0:
            rowp, *keep = pl.pallas_call(
                row_kernel,
                out_shape=[vmem((1, ROWS), f32)] + shapes,
                in_specs=[whole()] * (4 + KEPT),
                out_specs=[whole()] * (1 + KEPT),
                input_output_aliases={4 + k: 1 + k for k in range(KEPT)},
                scratch_shapes=[vmem((GROUPS, 128), f32), vmem((ROWS, 128), f32)],
                compiler_params=params(5),
                name="row",
            )(*parts, *map(in_vmem, keep))
        else:
            z0 = z_call(0, colp, feats, keep[1])
            rowp, z0, *keep = pl.pallas_call(
                row_z_kernel,
                out_shape=[vmem((1, ROWS), f32)] * 2 + shapes,
                in_specs=[whole()] * (5 + KEPT),
                out_specs=[whole()] * (2 + KEPT),
                input_output_aliases={5 + k: 2 + k for k in range(KEPT)},
                scratch_shapes=[vmem((GROUPS, 128), f32), vmem((ROWS, 128), f32)],
                compiler_params=params(5),
                name="row",
            )(*parts, in_vmem(z0), *map(in_vmem, keep))
        rowps = row_terms(rowp)
        colp, *keep = pl.pallas_call(
            col_kernel,
            out_shape=[vmem((GROUPS, 128), f32)] + shapes,
            in_specs=[whole()] * (4 + len(keep)),
            out_specs=[whole()] * (1 + len(keep)),
            input_output_aliases={4 + k: 1 + k for k in range(len(keep))},
            scratch_shapes=[vmem((ROWS, 128), f32)],
            compiler_params=params(5),
            name="col",
        )(*rowps, *map(in_vmem, keep))

    colsc, rzp, *keep = pl.pallas_call(
        last_row_kernel,
        out_shape=[vmem((GROUPS, 128), f32), vmem((2, ROWS), f32)] + shapes,
        in_specs=[whole()] * (6 + KEPT),
        out_specs=[whole()] * (2 + KEPT),
        input_output_aliases={6 + k: 2 + k for k in range(KEPT)},
        scratch_shapes=[vmem((ROWS, 128), f32)],
        compiler_params=params(5),
        name="row_last",
    )(*parts, in_vmem(z0), in_vmem(z1), *map(in_vmem, keep))
    terms = row_terms(rzp)
    pt, cb, token = pl.pallas_call(
        prep_kernel,
        out_shape=(vmem((OWN, D), bf16), vmem((OWN, 128), f32), vmem((8, 128), f32)),
        in_specs=[whole()] * 3,
        out_specs=(whole(),) * 3,
        compiler_params=params(5),
        name="prep",
    )(terms[0], in_vmem(colsc), in_vmem(keep[1]))
    rz = pl.pallas_call(
        rz_kernel,
        out_shape=vmem((2, ROWS), f32),
        in_specs=[whole()] * 5,
        out_specs=whole(),
        compiler_params=params(5),
        name="rz",
    )(*terms, token)
    rz_y = around(rz, "y")

    half = ROWS // 2
    mine, other = pl.pallas_call(
        dz_kernel,
        out_shape=(vmem((half, D), f32), vmem((half, D), f32)),
        in_specs=[whole()] * 5,
        out_specs=(whole(), whole()),
        scratch_shapes=[vmem((ROWS, 128), f32)] * 2 + [vmem((ROWS, D), f32)],
        compiler_params=params(5),
        name="dz",
    )(in_vmem(rz), in_vmem(colsc), in_vmem(feats), *map(in_vmem, keep))

    rz_rows, other = pl.pallas_call(
        stack_kernel,
        out_shape=(vmem((4, 2, ROWS), f32), vmem((half, D), f32)),
        in_specs=[whole()] * 5,
        out_specs=(whole(), whole()),
        input_output_aliases={4: 1},
        compiler_params=params(5),
        name="stack",
    )(*rz_y, other)
    rz_all = around(rz_rows, "x")

    got = lax.ppermute(other, "c", [(0, 1), (1, 0)])
    parts = around(mine + got, "z")

    proto_grad = pl.pallas_call(
        pg_kernel,
        grid=(NB * ROWS // PG_ROWS,),
        out_shape=sds((D, OWN), f32),
        in_specs=[whole()] * 6 + [pl.BlockSpec((PG_ROWS, 2 * D), lambda i: (i, 0))],
        out_specs=pl.BlockSpec((D, OWN), lambda i: (0, 0)),
        scratch_shapes=[
            vmem((OWN, D), f32),
            vmem((OWN, PG_ROWS), bf16),
            vmem((NB, 2, ROWS), f32),
        ],
        compiler_params=params(30),
        cost_estimate=pl.CostEstimate(flops=9700000000, bytes_accessed=8000000, transcendentals=12600000),
        name="pg",
    )(*rz_all, in_vmem(pt), in_vmem(cb), in_hbm(feats_all))

    parts, proto_grad, student_feats = lax.optimization_barrier(
        (parts, proto_grad, student_feats)
    )
    grad = pl.pallas_call(
        end_kernel,
        out_shape=vmem((half, D), f32),
        in_specs=[whole()] * 5,
        out_specs=whole(),
        compiler_params=params(5),
        name="feat_end",
    )(*parts, student_feats)
    feat_grad = pl.pallas_call(
        place_kernel,
        out_shape=sds((ROWS, D), f32),
        in_specs=[whole()] * 2,
        out_specs=whole(),
        compiler_params=params(5),
        name="feat_place",
    )(grad, lax.ppermute(grad, "c", [(0, 1), (1, 0)]))
    return (feat_grad, proto_grad)


def solution(mesh):
    grid = Mesh(mesh.devices.reshape(4, 4, 4, 2), ("x", "y", "z", "c"))
    in_specs = (P(XY, None), P(XY, None), P(None, ZC))
    out_specs = (P(XY, None), P(None, ZC + XY))
    return jax.shard_map(shards, mesh=grid, in_specs=in_specs, out_specs=out_specs, check_vma=False)
```

```python
import functools
import math

import jax
import jax.numpy as jnp
from jax import lax
from jax.experimental import pallas as pl
from jax.experimental.pallas import tpu as pltpu
from jax.sharding import Mesh, PartitionSpec as P

D = 256
PROTOS = 131072
ITERS = 3
ROWS = 384
COLS = 16384
OWN = 1024
SHARE = 48
BLOCK = 8192
PG_ROWS = 3072
CHUNK = 2048
KEPT = 2
GROUPS = COLS // 128
NB = 16
KT = math.log2(math.e) / 0.07
KS = math.log2(math.e) / 0.1
GSCALE = PROTOS / 0.1

f32 = jnp.float32
bf16 = jnp.bfloat16
XY = ("x", "y")
ZC = ("z", "c")
ALL = XY + ZC
MIB = 2**20


def whole():
    return pl.BlockSpec(memory_space=pltpu.VMEM)


def params(mib):
    return pltpu.CompilerParams(vmem_limit_bytes=mib * MIB)


def row_norm(feats):
    return lax.rsqrt(jnp.mean(feats * feats, axis=1, keepdims=True) + 1e-06) / math.sqrt(D)


def lanes_to_rows(vec, width):
    return jnp.transpose(jnp.broadcast_to(vec, (width, vec.shape[1])))


def rows_to_lanes(acc):
    return jnp.sum(jnp.transpose(acc), axis=0, keepdims=True)


def norm_kernel(t_ref, s_ref, out_ref, share_ref):
    for src, rows in ((t_ref, slice(0, ROWS)), (s_ref, slice(ROWS, 2 * ROWS))):
        feats = src[...].astype(f32)
        out_ref[rows, :] = (feats * row_norm(feats)).astype(bf16)
    start = (lax.axis_index("z") * 2 + lax.axis_index("c")) * SHARE
    for k in range(2):
        rows = pl.ds(pl.multiple_of(k * ROWS + start, SHARE), SHARE)
        share_ref[:, k * D : (k + 1) * D] = out_ref[rows, :]


def first_kernel(w_ref, f_ref, p_ref, e_ref, col_ref, sems):
    count = COLS // CHUNK

    def fetch(k):
        lanes = pl.ds(pl.multiple_of(k * CHUNK, CHUNK), CHUNK)
        return pltpu.make_async_copy(w_ref.at[:, lanes], p_ref.at[k], sems.at[k])

    for k in range(count):
        fetch(k).start()

    @pl.loop(0, count)
    def _(k):
        fetch(k).wait()
        sums = []
        for n in range(CHUNK // 256):
            lanes = slice(n * 256, (n + 1) * 256)
            w = p_ref[k, :, lanes].astype(f32)
            inv = lax.rsqrt(jnp.mean(w * w, axis=0, keepdims=True) + 1e-06) / math.sqrt(D)
            p = (w * inv).astype(bf16)
            p_ref[k, :, lanes] = p
            e = jnp.exp2(jnp.dot(f_ref[:ROWS, :], p, preferred_element_type=f32) * KT)
            e_ref[:, pl.ds(pl.multiple_of(k * CHUNK + n * 256, 256), 256)] = e
            for h in range(2):
                sums.append(jnp.sum(e[:, h * 128 : (h + 1) * 128], axis=0, keepdims=True))
        tall = CHUNK // 128
        col_ref[pl.ds(pl.multiple_of(k * tall, tall), tall), :] = jnp.concatenate(sums, axis=0)


def z_kernel(half, after_ref, f_ref, p_ref, z_ref):
    pairs = COLS // CHUNK // 4

    def body(k, zsum):
        for m in range(2):
            chunk = (half * pairs + k) * 2 + m
            for n in range(CHUNK // 256):
                p = p_ref[chunk, :, n * 256 : (n + 1) * 256]
                s = jnp.exp2(jnp.dot(f_ref[ROWS:, :], p, preferred_element_type=f32) * KS)
                zsum = zsum + s[:, :128] + s[:, 128:]
        return zsum

    z_ref[...] = rows_to_lanes(lax.fori_loop(0, pairs, body, jnp.zeros((ROWS, 128), f32)))


def sum_kernel(a_ref, b_ref, c_ref, d_ref, out_ref):
    out_ref[...] = (a_ref[...] + b_ref[...]) + (c_ref[...] + d_ref[...])


def pair_kernel(a_ref, b_ref, out_ref):
    out_ref[...] = a_ref[...] + b_ref[...]


def prep_kernel(after_ref, c_ref, p_ref, pt_ref, cb_ref, done_ref):
    x = lax.axis_index("x")
    y = lax.axis_index("y")
    block, per = x * 4 + y, CHUNK // OWN
    lanes = pl.ds(pl.multiple_of(lax.rem(block, per) * OWN, OWN), OWN)
    pt_ref[...] = jnp.transpose(p_ref[lax.div(block, per), :, lanes].astype(f32)).astype(bf16)
    own = c_ref[pl.ds(pl.multiple_of(block * 8, 8), 8), :]
    for q in range(8):
        cb_ref[q * 128 : (q + 1) * 128, :] = lanes_to_rows(own[q : q + 1, :], 128)
    done_ref[...] = jnp.zeros_like(done_ref)


def rz_kernel(a_ref, b_ref, c_ref, d_ref, after_ref, out_ref):
    out_ref[...] = GSCALE / ((a_ref[...] + b_ref[...]) + (c_ref[...] + d_ref[...]))


def stack_kernel(a_ref, b_ref, c_ref, d_ref, other_ref, out_ref, kept_ref):
    for d, ref in enumerate((a_ref, b_ref, c_ref, d_ref)):
        out_ref[d] = ref[...]


def sum_z_kernel(a_ref, b_ref, c_ref, d_ref, z_ref, out_ref, z_out):
    out_ref[...] = (a_ref[...] + b_ref[...]) + (c_ref[...] + d_ref[...])
    z_out[...] = z_ref[...]


def row_pass(cols, e_ref, c_ref, acc_ref):
    c_ref[...] = 1.0 / ((cols[0][...] + cols[1][...]) + (cols[2][...] + cols[3][...]))
    tiles = 12

    @pl.loop(0, ROWS // (8 * tiles))
    def _(k):
        base = pl.multiple_of(k * 8 * tiles, 8 * tiles)

        def body(q, accs):
            c8 = c_ref[pl.ds(pl.multiple_of(q * 8, 8), 8), :]
            cs = [jnp.broadcast_to(c8[u : u + 1, :], (8, 128)) for u in range(8)]
            out = []
            for i in range(tiles):
                e = e_ref[
                    pl.ds(pl.multiple_of(base + i * 8, 8), 8),
                    pl.ds(pl.multiple_of(q * 1024, 1024), 1024),
                ]
                p = [e[:, u * 128 : (u + 1) * 128] * cs[u] for u in range(8)]
                while len(p) > 1:
                    p = [p[m] + p[m + 1] for m in range(0, len(p), 2)]
                out.append(accs[i] + p[0])
            return tuple(out)

        zero = jnp.zeros((8, 128), f32)
        accs = lax.fori_loop(0, GROUPS // 8, body, (zero,) * tiles)
        for i in range(tiles):
            acc_ref[pl.ds(pl.multiple_of(base + i * 8, 8), 8), :] = accs[i]

    return rows_to_lanes(acc_ref[...])


def last_row_kernel(c0, c1, c2, c3, z0_ref, z1_ref, *refs):
    e_ref, (c_ref, row_ref), acc = refs[0], refs[KEPT : KEPT + 2], refs[-1]
    row = row_pass((c0, c1, c2, c3), e_ref, c_ref, acc)
    row_ref[...] = jnp.concatenate([row, z0_ref[...] + z1_ref[...]], axis=0)


def row_kernel(c0, c1, c2, c3, *refs):
    e_ref, row_ref, (c_ref, acc) = refs[0], refs[KEPT], refs[-2:]
    row_ref[...] = row_pass((c0, c1, c2, c3), e_ref, c_ref, acc)


def row_z_kernel(c0, c1, c2, c3, z_ref, *refs):
    e_ref, (row_ref, z_out), (c_ref, acc) = refs[0], refs[KEPT : KEPT + 2], refs[-2:]
    row_ref[...] = row_pass((c0, c1, c2, c3), e_ref, c_ref, acc)
    z_out[...] = z_ref[...]


def col_kernel(r0, r1, r2, r3, *refs):
    e_ref, col_ref, rb = refs[0], refs[len(refs) // 2 - 1], refs[-1]
    rb[...] = lanes_to_rows(1.0 / ((r0[...] + r1[...]) + (r2[...] + r3[...])), 128)

    @pl.loop(0, GROUPS // 8)
    def _(q):
        accs = [jnp.zeros((8, 128), f32) for _ in range(8)]
        for i in range(ROWS // 8):
            r = rb[i * 8 : (i + 1) * 8, :]
            e = e_ref[i * 8 : (i + 1) * 8, pl.ds(pl.multiple_of(q * 1024, 1024), 1024)]
            for u in range(8):
                accs[u] = accs[u] + e[:, u * 128 : (u + 1) * 128] * r
        part = jnp.concatenate([jnp.sum(a, axis=0, keepdims=True) for a in accs], axis=0)
        col_ref[pl.ds(pl.multiple_of(q * 8, 8), 8), :] = part


def dz_kernel(rz_ref, c_ref, f_ref, e_ref, p_ref, mine_ref, other_ref, rb, zb, dz_ref):
    rb[...] = lanes_to_rows(rz_ref[0:1, :], 128)
    zb[...] = lanes_to_rows(rz_ref[1:2, :], 128)
    dz_ref[...] = jnp.zeros_like(dz_ref)
    tall = BLOCK // 128

    @pl.loop(0, COLS // BLOCK)
    def _(k):
        cs = c_ref[pl.ds(pl.multiple_of(k * tall, tall), tall), :]
        r = rb[...]
        z = zb[...]
        acc = dz_ref[...]
        for n in range(BLOCK // 256):
            m, at = divmod(n * 256, CHUNK)
            p = p_ref[k * (BLOCK // CHUNK) + m, :, at : at + 256]
            s = jnp.exp2(jnp.dot(f_ref[ROWS:, :], p, preferred_element_type=f32) * KS)
            e = e_ref[:, pl.ds(pl.multiple_of(k * BLOCK + n * 256, 256), 256)]
            parts = []
            for h in range(2):
                lane = slice(h * 128, (h + 1) * 128)
                u = n * 2 + h
                parts.append((s[:, lane] * z - e[:, lane] * r * cs[u : u + 1, :]).astype(bf16))
            g = jnp.concatenate(parts, axis=1)
            acc = acc + lax.dot_general(
                g, p, (((1,), (1,)), ((), ())), preferred_element_type=f32
            )
        dz_ref[...] = acc

    half = ROWS // 2
    core = lax.axis_index("c")
    mine_ref[...] = dz_ref[pl.ds(pl.multiple_of(core * half, half), half), :]
    other_ref[...] = dz_ref[pl.ds(pl.multiple_of((1 - core) * half, half), half), :]


def joined_kernel(a_ref, b_ref, acc_ref, out_ref, kept_ref):
    out_ref[...] = a_ref[...] + b_ref[...]


def pg_kernel(part, r0, r1, r2, r3, pt, cb, f_ref, *refs):
    out_ref, g, rz = refs[-3:]
    x = lax.axis_index("x")
    y = lax.axis_index("y")
    for dx, ref in enumerate((r0, r1, r2, r3)):
        for dy in range(4):
            rz[lax.rem(x - dx + 4, 4) * 4 + lax.rem(y - dy + 4, 4)] = ref[dy]

    t = f_ref[:, :D]
    s = f_ref[:, D:]
    blocks = range(PG_ROWS // ROWS)
    rzs = [rz[part * len(blocks) + b] for b in blocks]
    r = jnp.concatenate([v[0:1, :] for v in rzs], axis=1)
    z = jnp.concatenate([v[1:2, :] for v in rzs], axis=1)
    nt = (((1,), (1,)), ((), ()))
    for n in range(PG_ROWS // 256):
        rows = slice(n * 256, (n + 1) * 256)
        et = jnp.exp2(lax.dot_general(pt[...], t[rows], nt, preferred_element_type=f32) * KT)
        es = jnp.exp2(lax.dot_general(pt[...], s[rows], nt, preferred_element_type=f32) * KS)
        for h in range(2):
            lane = slice(h * 128, (h + 1) * 128)
            to = slice(n * 256 + h * 128, n * 256 + (h + 1) * 128)
            g[:, to] = (es[:, lane] * z[:, to] - et[:, lane] * r[:, to] * cb[...]).astype(bf16)
    term = jnp.dot(g[...], s, preferred_element_type=f32)
    if part == 0:
        out_ref[...] = term
    else:
        out_ref[...] = jnp.transpose(refs[0][...] + term)


def end_kernel(a_ref, b_ref, s_ref, out_ref):
    half = ROWS // 2
    start = lax.axis_index("c") * half
    feats = s_ref[pl.ds(pl.multiple_of(start, half), half), :].astype(f32)
    rnorm = row_norm(feats)
    stud_f = feats * rnorm
    dz = a_ref[...] + b_ref[...]
    out_ref[...] = (dz - stud_f * jnp.sum(stud_f * dz, axis=1, keepdims=True)) * rnorm


def place_kernel(own_ref, sibling_ref, out_ref):
    half = ROWS // 2
    core = lax.axis_index("c")
    out_ref[pl.ds(pl.multiple_of(core * half, half), half), :] = own_ref[...]
    out_ref[pl.ds(pl.multiple_of((1 - core) * half, half), half), :] = sibling_ref[...]


def in_vmem(x):
    return pltpu.with_memory_space_constraint(x, pltpu.VMEM)


def in_hbm(x):
    return pltpu.with_memory_space_constraint(x, pltpu.HBM)


def around(x, axis):
    parts = [x]
    for d in (1, 2, 3):
        parts.append(lax.ppermute(x, axis, [(i, (i + d) % 4) for i in range(4)]))
    return parts


def row_terms(rowp):
    pair = pl.pallas_call(
        pair_kernel,
        out_shape=pltpu.VMEM(rowp.shape, f32),
        in_specs=[whole()] * 2,
        out_specs=whole(),
        compiler_params=params(5),
        name="pair",
    )(rowp, lax.ppermute(rowp, "c", [(0, 1), (1, 0)]))
    return around(pair, "z")


def z_call(half, after, feats, protos):
    return pl.pallas_call(
        functools.partial(z_kernel, half),
        out_shape=pltpu.VMEM((1, ROWS), f32),
        in_specs=[whole()] * 3,
        out_specs=whole(),
        compiler_params=params(5),
        name="zden",
    )(after, in_vmem(feats), in_vmem(protos))


def shards(teacher_feats, student_feats, proto_weight):
    sds = jax.ShapeDtypeStruct
    vmem = pltpu.VMEM
    kept = vmem((ROWS, COLS), f32)

    feats, share = pl.pallas_call(
        norm_kernel,
        grid=(1,),
        out_shape=(vmem((2 * ROWS, D), bf16), sds((SHARE, 2 * D), bf16)),
        in_specs=[pl.BlockSpec((ROWS, D), lambda i: (0, 0))] * 2,
        out_specs=(whole(), whole()),
        compiler_params=params(5),
        name="norm",
    )(in_hbm(teacher_feats), in_hbm(student_feats))
    feats_all = lax.all_gather(share, ALL, axis=0, tiled=True)

    packed = vmem((COLS // CHUNK, D, CHUNK), bf16)
    protos, expo, colp = pl.pallas_call(
        first_kernel,
        out_shape=(packed, kept, vmem((GROUPS, 128), f32)),
        in_specs=[pl.BlockSpec(memory_space=pl.ANY), whole()],
        out_specs=(whole(), whole(), whole()),
        scratch_shapes=[pltpu.SemaphoreType.DMA((COLS // CHUNK,))],
        compiler_params=params(5),
        name="first",
    )(in_hbm(proto_weight), in_vmem(feats))

    keep = [expo, protos]
    shapes = [kept, packed]
    for step in range(ITERS):
        parts = around(colp, "y")
        if step == 2:
            z1 = z_call(1, colp, feats, keep[1])
            colp, z1 = pl.pallas_call(
                sum_z_kernel,
                out_shape=(vmem((GROUPS, 128), f32), vmem((1, ROWS), f32)),
                in_specs=[whole()] * 5,
                out_specs=(whole(), whole()),
                compiler_params=params(5),
                name="sum_z",
            )(*parts, z1)
        else:
            colp = pl.pallas_call(
                sum_kernel,
                out_shape=vmem((GROUPS, 128), f32),
                in_specs=[whole()] * 4,
                out_specs=whole(),
                compiler_params=params(5),
                name="sum",
            )(*parts)
        parts = around(colp, "x")
        if step == 2:
            break
        if step == 0:
            rowp, *keep = pl.pallas_call(
                row_kernel,
                out_shape=[vmem((1, ROWS), f32)] + shapes,
                in_specs=[whole()] * (4 + KEPT),
                out_specs=[whole()] * (1 + KEPT),
                input_output_aliases={4 + k: 1 + k for k in range(KEPT)},
                scratch_shapes=[vmem((GROUPS, 128), f32), vmem((ROWS, 128), f32)],
                compiler_params=params(5),
                name="row",
            )(*parts, *map(in_vmem, keep))
        else:
            z0 = z_call(0, colp, feats, keep[1])
            rowp, z0, *keep = pl.pallas_call(
                row_z_kernel,
                out_shape=[vmem((1, ROWS), f32)] * 2 + shapes,
                in_specs=[whole()] * (5 + KEPT),
                out_specs=[whole()] * (2 + KEPT),
                input_output_aliases={5 + k: 2 + k for k in range(KEPT)},
                scratch_shapes=[vmem((GROUPS, 128), f32), vmem((ROWS, 128), f32)],
                compiler_params=params(5),
                name="row",
            )(*parts, in_vmem(z0), *map(in_vmem, keep))
        rowps = row_terms(rowp)
        colp, *keep = pl.pallas_call(
            col_kernel,
            out_shape=[vmem((GROUPS, 128), f32)] + shapes,
            in_specs=[whole()] * (4 + len(keep)),
            out_specs=[whole()] * (1 + len(keep)),
            input_output_aliases={4 + k: 1 + k for k in range(len(keep))},
            scratch_shapes=[vmem((ROWS, 128), f32)],
            compiler_params=params(5),
            name="col",
        )(*rowps, *map(in_vmem, keep))

    colsc, rzp, *keep = pl.pallas_call(
        last_row_kernel,
        out_shape=[vmem((GROUPS, 128), f32), vmem((2, ROWS), f32)] + shapes,
        in_specs=[whole()] * (6 + KEPT),
        out_specs=[whole()] * (2 + KEPT),
        input_output_aliases={6 + k: 2 + k for k in range(KEPT)},
        scratch_shapes=[vmem((ROWS, 128), f32)],
        compiler_params=params(5),
        name="row_last",
    )(*parts, in_vmem(z0), in_vmem(z1), *map(in_vmem, keep))
    terms = row_terms(rzp)
    pt, cb, token = pl.pallas_call(
        prep_kernel,
        out_shape=(vmem((OWN, D), bf16), vmem((OWN, 128), f32), vmem((8, 128), f32)),
        in_specs=[whole()] * 3,
        out_specs=(whole(),) * 3,
        compiler_params=params(5),
        name="prep",
    )(terms[0], in_vmem(colsc), in_vmem(keep[1]))
    rz = pl.pallas_call(
        rz_kernel,
        out_shape=vmem((2, ROWS), f32),
        in_specs=[whole()] * 5,
        out_specs=whole(),
        compiler_params=params(5),
        name="rz",
    )(*terms, token)
    rz_y = around(rz, "y")

    half = ROWS // 2
    mine, other = pl.pallas_call(
        dz_kernel,
        out_shape=(vmem((half, D), f32), vmem((half, D), f32)),
        in_specs=[whole()] * 5,
        out_specs=(whole(), whole()),
        scratch_shapes=[vmem((ROWS, 128), f32)] * 2 + [vmem((ROWS, D), f32)],
        compiler_params=params(5),
        name="dz",
    )(in_vmem(rz), in_vmem(colsc), in_vmem(feats), *map(in_vmem, keep))

    rz_rows, other = pl.pallas_call(
        stack_kernel,
        out_shape=(vmem((4, 2, ROWS), f32), vmem((half, D), f32)),
        in_specs=[whole()] * 5,
        out_specs=(whole(), whole()),
        input_output_aliases={4: 1},
        compiler_params=params(5),
        name="stack",
    )(*rz_y, other)
    rz_all = around(rz_rows, "x")

    got = lax.ppermute(other, "c", [(0, 1), (1, 0)])
    dz = mine + got
    beside = lax.ppermute(dz, "z", [(i, i ^ 1) for i in range(4)])

    def pg(part, out, *acc):
        return pl.pallas_call(
            functools.partial(pg_kernel, part),
            grid=(1,),
            out_shape=out,
            in_specs=[whole()] * 6
            + [pl.BlockSpec((PG_ROWS, 2 * D), lambda i: (part, 0))]
            + [whole()] * len(acc),
            out_specs=whole(),
            scratch_shapes=[vmem((OWN, PG_ROWS), bf16), vmem((NB, 2, ROWS), f32)],
            compiler_params=params(26),
            cost_estimate=pl.CostEstimate(
                flops=4850000000, bytes_accessed=4000000, transcendentals=6300000
            ),
            name="pg",
        )(*rz_all, in_vmem(pt), in_vmem(cb), in_hbm(feats_all), *acc)

    acc = pg(0, vmem((OWN, D), f32))
    dz, acc = pl.pallas_call(
        joined_kernel,
        out_shape=(vmem((half, D), f32), vmem((OWN, D), f32)),
        in_specs=[whole()] * 3,
        out_specs=(whole(), whole()),
        input_output_aliases={2: 1},
        compiler_params=params(26),
        name="joined",
    )(dz, beside, in_vmem(acc))
    parts = (dz, lax.ppermute(dz, "z", [(i, i ^ 3) for i in range(4)]))
    proto_grad = pg(1, sds((D, OWN), f32), in_vmem(acc))

    parts, proto_grad, student_feats = lax.optimization_barrier(
        (parts, proto_grad, student_feats)
    )
    grad = pl.pallas_call(
        end_kernel,
        out_shape=vmem((half, D), f32),
        in_specs=[whole()] * 3,
        out_specs=whole(),
        compiler_params=params(5),
        name="feat_end",
    )(*parts, student_feats)
    feat_grad = pl.pallas_call(
        place_kernel,
        out_shape=sds((ROWS, D), f32),
        in_specs=[whole()] * 2,
        out_specs=whole(),
        compiler_params=params(5),
        name="feat_place",
    )(grad, lax.ppermute(grad, "c", [(0, 1), (1, 0)]))
    return (feat_grad, proto_grad)


def solution(mesh):
    grid = Mesh(mesh.devices.reshape(4, 4, 4, 2), ("x", "y", "z", "c"))
    in_specs = (P(XY, None), P(XY, None), P(None, ZC))
    out_specs = (P(XY, None), P(None, ZC + XY))
    return jax.shard_map(shards, mesh=grid, in_specs=in_specs, out_specs=out_specs, check_vma=False)
```

```python
import functools
import math

import jax
import jax.numpy as jnp
from jax import lax
from jax.experimental import pallas as pl
from jax.experimental.pallas import tpu as pltpu
from jax.sharding import Mesh, PartitionSpec as P

D = 256
PROTOS = 131072
ITERS = 3
ROWS = 384
COLS = 16384
OWN = 1024
SHARE = 48
BLOCK = 8192
PG_ROWS = 3072
CHUNK = 2048
KEPT = 2
GROUPS = COLS // 128
NB = 16
KT = math.log2(math.e) / 0.07
KS = math.log2(math.e) / 0.1
GSCALE = PROTOS / 0.1

f32 = jnp.float32
bf16 = jnp.bfloat16
XY = ("x", "y")
ZC = ("z", "c")
ALL = XY + ZC
MIB = 2**20


def whole():
    return pl.BlockSpec(memory_space=pltpu.VMEM)


def params(mib):
    return pltpu.CompilerParams(vmem_limit_bytes=mib * MIB)


def row_norm(feats):
    return lax.rsqrt(jnp.mean(feats * feats, axis=1, keepdims=True) + 1e-06) / math.sqrt(D)


def lanes_to_rows(vec, width):
    return jnp.transpose(jnp.broadcast_to(vec, (width, vec.shape[1])))


def rows_to_lanes(acc):
    return jnp.sum(jnp.transpose(acc), axis=0, keepdims=True)


def norm_kernel(t_ref, s_ref, w_ref, out_ref, share_ref, w0_ref, sem):
    copy = pltpu.make_async_copy(w_ref.at[:, pl.ds(0, CHUNK)], w0_ref, sem)
    copy.start()
    for src, rows in ((t_ref, slice(0, ROWS)), (s_ref, slice(ROWS, 2 * ROWS))):
        feats = src[...].astype(f32)
        out_ref[rows, :] = (feats * row_norm(feats)).astype(bf16)
    start = (lax.axis_index("z") * 2 + lax.axis_index("c")) * SHARE
    for k in range(2):
        rows = pl.ds(pl.multiple_of(k * ROWS + start, SHARE), SHARE)
        share_ref[:, k * D : (k + 1) * D] = out_ref[rows, :]
    copy.wait()


def first_kernel(w_ref, w0_ref, f_ref, p_ref, e_ref, col_ref, sems):
    count = COLS // CHUNK

    def fetch(k):
        lanes = pl.ds(pl.multiple_of(k * CHUNK, CHUNK), CHUNK)
        return pltpu.make_async_copy(w_ref.at[:, lanes], p_ref.at[k], sems.at[k])

    pltpu.make_async_copy(w0_ref, p_ref.at[0], sems.at[0]).start()
    for k in range(1, count):
        fetch(k).start()

    @pl.loop(0, count)
    def _(k):
        fetch(k).wait()
        sums = []
        for n in range(CHUNK // 256):
            lanes = slice(n * 256, (n + 1) * 256)
            w = p_ref[k, :, lanes].astype(f32)
            inv = lax.rsqrt(jnp.mean(w * w, axis=0, keepdims=True) + 1e-06) / math.sqrt(D)
            p = (w * inv).astype(bf16)
            p_ref[k, :, lanes] = p
            e = jnp.exp2(jnp.dot(f_ref[:ROWS, :], p, preferred_element_type=f32) * KT)
            e_ref[:, pl.ds(pl.multiple_of(k * CHUNK + n * 256, 256), 256)] = e
            for h in range(2):
                sums.append(jnp.sum(e[:, h * 128 : (h + 1) * 128], axis=0, keepdims=True))
        tall = CHUNK // 128
        col_ref[pl.ds(pl.multiple_of(k * tall, tall), tall), :] = jnp.concatenate(sums, axis=0)


def z_kernel(half, after_ref, f_ref, p_ref, z_ref):
    pairs = COLS // CHUNK // 4

    def body(k, zsum):
        for m in range(2):
            chunk = (half * pairs + k) * 2 + m
            for n in range(CHUNK // 256):
                p = p_ref[chunk, :, n * 256 : (n + 1) * 256]
                s = jnp.exp2(jnp.dot(f_ref[ROWS:, :], p, preferred_element_type=f32) * KS)
                zsum = zsum + s[:, :128] + s[:, 128:]
        return zsum

    z_ref[...] = rows_to_lanes(lax.fori_loop(0, pairs, body, jnp.zeros((ROWS, 128), f32)))


def sum_kernel(a_ref, b_ref, c_ref, d_ref, out_ref):
    out_ref[...] = (a_ref[...] + b_ref[...]) + (c_ref[...] + d_ref[...])


def pair_kernel(a_ref, b_ref, out_ref):
    out_ref[...] = a_ref[...] + b_ref[...]


def prep_kernel(after_ref, c_ref, p_ref, pt_ref, cb_ref, done_ref):
    x = lax.axis_index("x")
    y = lax.axis_index("y")
    block, per = x * 4 + y, CHUNK // OWN
    lanes = pl.ds(pl.multiple_of(lax.rem(block, per) * OWN, OWN), OWN)
    pt_ref[...] = jnp.transpose(p_ref[lax.div(block, per), :, lanes].astype(f32)).astype(bf16)
    own = c_ref[pl.ds(pl.multiple_of(block * 8, 8), 8), :]
    for q in range(8):
        cb_ref[q * 128 : (q + 1) * 128, :] = lanes_to_rows(own[q : q + 1, :], 128)
    done_ref[...] = jnp.zeros_like(done_ref)


def rz_kernel(a_ref, b_ref, c_ref, d_ref, after_ref, out_ref):
    out_ref[...] = GSCALE / ((a_ref[...] + b_ref[...]) + (c_ref[...] + d_ref[...]))


def stack_kernel(a_ref, b_ref, c_ref, d_ref, other_ref, out_ref, kept_ref):
    for d, ref in enumerate((a_ref, b_ref, c_ref, d_ref)):
        out_ref[d] = ref[...]


def sum_z_kernel(a_ref, b_ref, c_ref, d_ref, z_ref, out_ref, z_out):
    out_ref[...] = (a_ref[...] + b_ref[...]) + (c_ref[...] + d_ref[...])
    z_out[...] = z_ref[...]


def row_pass(cols, e_ref, c_ref, acc_ref):
    c_ref[...] = 1.0 / ((cols[0][...] + cols[1][...]) + (cols[2][...] + cols[3][...]))
    tiles = 12

    @pl.loop(0, ROWS // (8 * tiles))
    def _(k):
        base = pl.multiple_of(k * 8 * tiles, 8 * tiles)

        def body(q, accs):
            c8 = c_ref[pl.ds(pl.multiple_of(q * 8, 8), 8), :]
            cs = [jnp.broadcast_to(c8[u : u + 1, :], (8, 128)) for u in range(8)]
            out = []
            for i in range(tiles):
                e = e_ref[
                    pl.ds(pl.multiple_of(base + i * 8, 8), 8),
                    pl.ds(pl.multiple_of(q * 1024, 1024), 1024),
                ]
                p = [e[:, u * 128 : (u + 1) * 128] * cs[u] for u in range(8)]
                while len(p) > 1:
                    p = [p[m] + p[m + 1] for m in range(0, len(p), 2)]
                out.append(accs[i] + p[0])
            return tuple(out)

        zero = jnp.zeros((8, 128), f32)
        accs = lax.fori_loop(0, GROUPS // 8, body, (zero,) * tiles)
        for i in range(tiles):
            acc_ref[pl.ds(pl.multiple_of(base + i * 8, 8), 8), :] = accs[i]

    return rows_to_lanes(acc_ref[...])


def last_row_kernel(c0, c1, c2, c3, z0_ref, z1_ref, *refs):
    e_ref, (c_ref, row_ref), acc = refs[0], refs[KEPT : KEPT + 2], refs[-1]
    row = row_pass((c0, c1, c2, c3), e_ref, c_ref, acc)
    row_ref[...] = jnp.concatenate([row, z0_ref[...] + z1_ref[...]], axis=0)


def row_kernel(c0, c1, c2, c3, *refs):
    e_ref, row_ref, (c_ref, acc) = refs[0], refs[KEPT], refs[-2:]
    row_ref[...] = row_pass((c0, c1, c2, c3), e_ref, c_ref, acc)


def row_z_kernel(c0, c1, c2, c3, z_ref, *refs):
    e_ref, (row_ref, z_out), (c_ref, acc) = refs[0], refs[KEPT : KEPT + 2], refs[-2:]
    row_ref[...] = row_pass((c0, c1, c2, c3), e_ref, c_ref, acc)
    z_out[...] = z_ref[...]


def col_kernel(r0, r1, r2, r3, *refs):
    e_ref, col_ref, rb = refs[0], refs[len(refs) // 2 - 1], refs[-1]
    rb[...] = lanes_to_rows(1.0 / ((r0[...] + r1[...]) + (r2[...] + r3[...])), 128)

    @pl.loop(0, GROUPS // 8)
    def _(q):
        accs = [jnp.zeros((8, 128), f32) for _ in range(8)]
        for i in range(ROWS // 8):
            r = rb[i * 8 : (i + 1) * 8, :]
            e = e_ref[i * 8 : (i + 1) * 8, pl.ds(pl.multiple_of(q * 1024, 1024), 1024)]
            for u in range(8):
                accs[u] = accs[u] + e[:, u * 128 : (u + 1) * 128] * r
        part = jnp.concatenate([jnp.sum(a, axis=0, keepdims=True) for a in accs], axis=0)
        col_ref[pl.ds(pl.multiple_of(q * 8, 8), 8), :] = part


def dz_kernel(rz_ref, c_ref, f_ref, e_ref, p_ref, mine_ref, other_ref, rb, zb, dz_ref):
    rb[...] = lanes_to_rows(rz_ref[0:1, :], 128)
    zb[...] = lanes_to_rows(rz_ref[1:2, :], 128)
    dz_ref[...] = jnp.zeros_like(dz_ref)
    tall = BLOCK // 128

    @pl.loop(0, COLS // BLOCK)
    def _(k):
        cs = c_ref[pl.ds(pl.multiple_of(k * tall, tall), tall), :]
        r = rb[...]
        z = zb[...]
        acc = dz_ref[...]
        for n in range(BLOCK // 256):
            m, at = divmod(n * 256, CHUNK)
            p = p_ref[k * (BLOCK // CHUNK) + m, :, at : at + 256]
            s = jnp.exp2(jnp.dot(f_ref[ROWS:, :], p, preferred_element_type=f32) * KS)
            e = e_ref[:, pl.ds(pl.multiple_of(k * BLOCK + n * 256, 256), 256)]
            parts = []
            for h in range(2):
                lane = slice(h * 128, (h + 1) * 128)
                u = n * 2 + h
                parts.append((s[:, lane] * z - e[:, lane] * r * cs[u : u + 1, :]).astype(bf16))
            g = jnp.concatenate(parts, axis=1)
            acc = acc + lax.dot_general(
                g, p, (((1,), (1,)), ((), ())), preferred_element_type=f32
            )
        dz_ref[...] = acc

    half = ROWS // 2
    core = lax.axis_index("c")
    mine_ref[...] = dz_ref[pl.ds(pl.multiple_of(core * half, half), half), :]
    other_ref[...] = dz_ref[pl.ds(pl.multiple_of((1 - core) * half, half), half), :]


def pg_kernel(r0, r1, r2, r3, pt, cb, f_ref, out_ref, acc, g, rz):
    step = pl.program_id(0)

    @pl.when(step == 0)
    def _():
        acc[...] = jnp.zeros_like(acc)
        x = lax.axis_index("x")
        y = lax.axis_index("y")
        for dx, ref in enumerate((r0, r1, r2, r3)):
            for dy in range(4):
                rz[lax.rem(x - dx + 4, 4) * 4 + lax.rem(y - dy + 4, 4)] = ref[dy]

    t = f_ref[:, :D]
    s = f_ref[:, D:]
    blocks = range(PG_ROWS // ROWS)
    rzs = [rz[step * len(blocks) + b] for b in blocks]
    r = jnp.concatenate([v[0:1, :] for v in rzs], axis=1)
    z = jnp.concatenate([v[1:2, :] for v in rzs], axis=1)
    nt = (((1,), (1,)), ((), ()))
    for n in range(PG_ROWS // 256):
        rows = slice(n * 256, (n + 1) * 256)
        et = jnp.exp2(lax.dot_general(pt[...], t[rows], nt, preferred_element_type=f32) * KT)
        es = jnp.exp2(lax.dot_general(pt[...], s[rows], nt, preferred_element_type=f32) * KS)
        for h in range(2):
            lane = slice(h * 128, (h + 1) * 128)
            to = slice(n * 256 + h * 128, n * 256 + (h + 1) * 128)
            g[:, to] = (es[:, lane] * z[:, to] - et[:, lane] * r[:, to] * cb[...]).astype(bf16)
    acc[...] += jnp.dot(g[...], s, preferred_element_type=f32)

    @pl.when(step == pl.num_programs(0) - 1)
    def _():
        out_ref[...] = jnp.transpose(acc[...])


def end_kernel(a_ref, b_ref, c_ref, d_ref, s_ref, out_ref):
    half = ROWS // 2
    start = lax.axis_index("c") * half
    feats = s_ref[pl.ds(pl.multiple_of(start, half), half), :].astype(f32)
    rnorm = row_norm(feats)
    stud_f = feats * rnorm
    dz = (a_ref[...] + c_ref[...]) + (b_ref[...] + d_ref[...])
    out_ref[...] = (dz - stud_f * jnp.sum(stud_f * dz, axis=1, keepdims=True)) * rnorm


def place_kernel(own_ref, sibling_ref, out_ref):
    half = ROWS // 2
    core = lax.axis_index("c")
    out_ref[pl.ds(pl.multiple_of(core * half, half), half), :] = own_ref[...]
    out_ref[pl.ds(pl.multiple_of((1 - core) * half, half), half), :] = sibling_ref[...]


def in_vmem(x):
    return pltpu.with_memory_space_constraint(x, pltpu.VMEM)


def in_hbm(x):
    return pltpu.with_memory_space_constraint(x, pltpu.HBM)


def around(x, axis):
    parts = [x]
    for d in (1, 2, 3):
        parts.append(lax.ppermute(x, axis, [(i, (i + d) % 4) for i in range(4)]))
    return parts


def row_terms(rowp):
    pair = pl.pallas_call(
        pair_kernel,
        out_shape=pltpu.VMEM(rowp.shape, f32),
        in_specs=[whole()] * 2,
        out_specs=whole(),
        compiler_params=params(5),
        name="pair",
    )(rowp, lax.ppermute(rowp, "c", [(0, 1), (1, 0)]))
    return around(pair, "z")


def z_call(half, after, feats, protos):
    return pl.pallas_call(
        functools.partial(z_kernel, half),
        out_shape=pltpu.VMEM((1, ROWS), f32),
        in_specs=[whole()] * 3,
        out_specs=whole(),
        compiler_params=params(5),
        name="zden",
    )(after, in_vmem(feats), in_vmem(protos))


def shards(teacher_feats, student_feats, proto_weight):
    sds = jax.ShapeDtypeStruct
    vmem = pltpu.VMEM
    kept = vmem((ROWS, COLS), f32)

    feats, share, w0 = pl.pallas_call(
        norm_kernel,
        grid=(1,),
        out_shape=(vmem((2 * ROWS, D), bf16), sds((SHARE, 2 * D), bf16), vmem((D, CHUNK), bf16)),
        in_specs=[pl.BlockSpec((ROWS, D), lambda i: (0, 0))] * 2
        + [pl.BlockSpec(memory_space=pl.ANY)],
        out_specs=(whole(),) * 3,
        scratch_shapes=[pltpu.SemaphoreType.DMA(())],
        compiler_params=params(5),
        name="norm",
    )(in_hbm(teacher_feats), in_hbm(student_feats), in_hbm(proto_weight))
    feats_all = lax.all_gather(share, ALL, axis=0, tiled=True)

    packed = vmem((COLS // CHUNK, D, CHUNK), bf16)
    protos, expo, colp = pl.pallas_call(
        first_kernel,
        out_shape=(packed, kept, vmem((GROUPS, 128), f32)),
        in_specs=[pl.BlockSpec(memory_space=pl.ANY), whole(), whole()],
        out_specs=(whole(), whole(), whole()),
        scratch_shapes=[pltpu.SemaphoreType.DMA((COLS // CHUNK,))],
        compiler_params=params(5),
        name="first",
    )(in_hbm(proto_weight), in_vmem(w0), in_vmem(feats))

    keep = [expo, protos]
    shapes = [kept, packed]
    for step in range(ITERS):
        parts = around(colp, "y")
        if step == 2:
            z1 = z_call(1, colp, feats, keep[1])
            colp, z1 = pl.pallas_call(
                sum_z_kernel,
                out_shape=(vmem((GROUPS, 128), f32), vmem((1, ROWS), f32)),
                in_specs=[whole()] * 5,
                out_specs=(whole(), whole()),
                compiler_params=params(5),
                name="sum_z",
            )(*parts, z1)
        else:
            colp = pl.pallas_call(
                sum_kernel,
                out_shape=vmem((GROUPS, 128), f32),
                in_specs=[whole()] * 4,
                out_specs=whole(),
                compiler_params=params(5),
                name="sum",
            )(*parts)
        parts = around(colp, "x")
        if step == 2:
            break
        if step == 0:
            rowp, *keep = pl.pallas_call(
                row_kernel,
                out_shape=[vmem((1, ROWS), f32)] + shapes,
                in_specs=[whole()] * (4 + KEPT),
                out_specs=[whole()] * (1 + KEPT),
                input_output_aliases={4 + k: 1 + k for k in range(KEPT)},
                scratch_shapes=[vmem((GROUPS, 128), f32), vmem((ROWS, 128), f32)],
                compiler_params=params(5),
                name="row",
            )(*parts, *map(in_vmem, keep))
        else:
            z0 = z_call(0, colp, feats, keep[1])
            rowp, z0, *keep = pl.pallas_call(
                row_z_kernel,
                out_shape=[vmem((1, ROWS), f32)] * 2 + shapes,
                in_specs=[whole()] * (5 + KEPT),
                out_specs=[whole()] * (2 + KEPT),
                input_output_aliases={5 + k: 2 + k for k in range(KEPT)},
                scratch_shapes=[vmem((GROUPS, 128), f32), vmem((ROWS, 128), f32)],
                compiler_params=params(5),
                name="row",
            )(*parts, in_vmem(z0), *map(in_vmem, keep))
        rowps = row_terms(rowp)
        colp, *keep = pl.pallas_call(
            col_kernel,
            out_shape=[vmem((GROUPS, 128), f32)] + shapes,
            in_specs=[whole()] * (4 + len(keep)),
            out_specs=[whole()] * (1 + len(keep)),
            input_output_aliases={4 + k: 1 + k for k in range(len(keep))},
            scratch_shapes=[vmem((ROWS, 128), f32)],
            compiler_params=params(5),
            name="col",
        )(*rowps, *map(in_vmem, keep))

    colsc, rzp, *keep = pl.pallas_call(
        last_row_kernel,
        out_shape=[vmem((GROUPS, 128), f32), vmem((2, ROWS), f32)] + shapes,
        in_specs=[whole()] * (6 + KEPT),
        out_specs=[whole()] * (2 + KEPT),
        input_output_aliases={6 + k: 2 + k for k in range(KEPT)},
        scratch_shapes=[vmem((ROWS, 128), f32)],
        compiler_params=params(5),
        name="row_last",
    )(*parts, in_vmem(z0), in_vmem(z1), *map(in_vmem, keep))
    terms = row_terms(rzp)
    pt, cb, token = pl.pallas_call(
        prep_kernel,
        out_shape=(vmem((OWN, D), bf16), vmem((OWN, 128), f32), vmem((8, 128), f32)),
        in_specs=[whole()] * 3,
        out_specs=(whole(),) * 3,
        compiler_params=params(5),
        name="prep",
    )(terms[0], in_vmem(colsc), in_vmem(keep[1]))
    rz = pl.pallas_call(
        rz_kernel,
        out_shape=vmem((2, ROWS), f32),
        in_specs=[whole()] * 5,
        out_specs=whole(),
        compiler_params=params(5),
        name="rz",
    )(*terms, token)
    rz_y = around(rz, "y")

    half = ROWS // 2
    mine, other = pl.pallas_call(
        dz_kernel,
        out_shape=(vmem((half, D), f32), vmem((half, D), f32)),
        in_specs=[whole()] * 5,
        out_specs=(whole(), whole()),
        scratch_shapes=[vmem((ROWS, 128), f32)] * 2 + [vmem((ROWS, D), f32)],
        compiler_params=params(5),
        name="dz",
    )(in_vmem(rz), in_vmem(colsc), in_vmem(feats), *map(in_vmem, keep))

    rz_rows, other = pl.pallas_call(
        stack_kernel,
        out_shape=(vmem((4, 2, ROWS), f32), vmem((half, D), f32)),
        in_specs=[whole()] * 5,
        out_specs=(whole(), whole()),
        input_output_aliases={4: 1},
        compiler_params=params(5),
        name="stack",
    )(*rz_y, other)
    rz_all = around(rz_rows, "x")

    got = lax.ppermute(other, "c", [(0, 1), (1, 0)])
    parts = around(mine + got, "z")

    proto_grad = pl.pallas_call(
        pg_kernel,
        grid=(NB * ROWS // PG_ROWS,),
        out_shape=sds((D, OWN), f32),
        in_specs=[whole()] * 6 + [pl.BlockSpec((PG_ROWS, 2 * D), lambda i: (i, 0))],
        out_specs=pl.BlockSpec((D, OWN), lambda i: (0, 0)),
        scratch_shapes=[
            vmem((OWN, D), f32),
            vmem((OWN, PG_ROWS), bf16),
            vmem((NB, 2, ROWS), f32),
        ],
        compiler_params=params(30),
        cost_estimate=pl.CostEstimate(flops=9700000000, bytes_accessed=8000000, transcendentals=12600000),
        name="pg",
    )(*rz_all, in_vmem(pt), in_vmem(cb), in_hbm(feats_all))

    parts, proto_grad, student_feats = lax.optimization_barrier(
        (parts, proto_grad, student_feats)
    )
    grad = pl.pallas_call(
        end_kernel,
        out_shape=vmem((half, D), f32),
        in_specs=[whole()] * 5,
        out_specs=whole(),
        compiler_params=params(5),
        name="feat_end",
    )(*parts, student_feats)
    feat_grad = pl.pallas_call(
        place_kernel,
        out_shape=sds((ROWS, D), f32),
        in_specs=[whole()] * 2,
        out_specs=whole(),
        compiler_params=params(5),
        name="feat_place",
    )(grad, lax.ppermute(grad, "c", [(0, 1), (1, 0)]))
    return (feat_grad, proto_grad)


def solution(mesh):
    grid = Mesh(mesh.devices.reshape(4, 4, 4, 2), ("x", "y", "z", "c"))
    in_specs = (P(XY, None), P(XY, None), P(None, ZC))
    out_specs = (P(XY, None), P(None, ZC + XY))
    return jax.shard_map(shards, mesh=grid, in_specs=in_specs, out_specs=out_specs, check_vma=False)
```
